32 devices in a mesh: groups: 2 (over y), expert: 4 (over z), dp: 2 (over x), head: 2 (over core).
Axes of the slice: x: 2, y: 2, z: 4, core: 2. Of those that a mesh axis runs over, the one named last changes fastest.
Arguments:
- queries: bfloat16 [32, 64, 128], P(('groups', 'expert', 'dp'), 'head'), parts along dimension 0, may hold values from -100 to 100
- new_key: bfloat16 [32, 4, 128], P(('groups', 'expert', 'dp'), 'head'), parts along dimension 0, may hold values from -4.5 to 4.5
- new_value: bfloat16 [32, 4, 128], P(('groups', 'expert', 'dp'), 'head'), parts along dimension 0, may hold values from -4.5 to 4.5
- key_cache: bfloat16 [32, 512, 4, 128], P(('groups', 'expert', 'dp'), None, 'head'), parts along dimension 0, may hold values from -4.5 to 4.5
- value_cache: bfloat16 [32, 512, 4, 128], P(('groups', 'expert', 'dp'), None, 'head'), parts along dimension 0, may hold values from -4.5 to 4.5
- lengths: int32 [32], P(('groups', 'expert', 'dp')), parts along dimension 0, may hold values from 2 to 512, as said below
- w_out: bfloat16 [8192, 4096], P('head', ('expert', 'dp')), may hold values from -0.0625 to 0.0625
- resid_cols: bfloat16 [32, 4096], P('groups', ('expert', 'dp')), parts along dimension 0, may hold values from -6 to 6
- norm_gain: float32 [4096], replicated, may hold values from 0.5 to 1.5
- router: bfloat16 [4096, 128], replicated, may hold values from -12 to 12
- routes: int32 [32, 8], P('groups'), parts along dimension 0, may hold values from 0 to 127, as said below
- capacity_slot: int32 [32], P('groups'), parts along dimension 0, may hold values from 0 to 3, as said below
- w_gate: bfloat16 [4, 4096, 1536], P('expert', 'head', 'dp'), may hold values from -0.09375 to 0.09375
- w_up: bfloat16 [4, 4096, 1536], P('expert', 'head', 'dp'), may hold values from -0.09375 to 0.09375
- w_down: bfloat16 [4, 1536, 4096], P('expert', 'dp', 'head'), may hold values from -0.15625 to 0.15625
Outputs:
- layer_out: bfloat16 [32, 4096], P(('groups', 'expert', 'dp'), 'head'), parts along dimension 0
The draws below stay inside these ranges and needn't reach their ends.
There are 2 independent parts, one for each index of `groups`. The reference program is written for one: setup_inputs(seed, part) draws one part's arguments, and reference() takes and returns one part's arrays. A program takes and returns all parts, laid end to end along the dimension named above; an argument that names none is the same for every part. Nothing has to cross between parts.
Inputs may be any that keep to these rules, and one draw needn't show every extreme that they name: `routes`: each row names 8 different experts; exactly one of them is below 4, at a position that varies from row to row, and the others are 4 or more. capacity_slot[r] is row r's place among the rows whose expert below 4 is the same; these places run from 0 to that expert's row count minus 1. No expert below 4 has more than 4 rows, and one has exactly 4. `lengths`: some row has exactly 512 cached tokens.
All inputs are finite; a program needn't handle non-finite values.
Results may differ from the reference program's by a relative error of at most 0.0033.
The reference program's roundings to bfloat16 on the way count: a program that leaves them out, or rounds other values in their place, can miss the bound.
Values may be sent and summed in bfloat16 or wider, within the bound.
A program may use at most 64 MiB of HBM per device.

```python
import math
import jax
import jax.numpy as jnp
from jax import lax

D = 4096
FF = 1536
EXPERTS = 128
TOP = 8
QH = 64
KVH = 4
HD = 128
CACHE = 512
FLIGHT = 4
ROWS = 16
CAP = 4


def shared_keys(key):
    return jnp.clip(jax.random.normal(key, (ROWS, CACHE, KVH, HD), jnp.float32), -4.5, 4.5)


def routing_plan(key):
    parts = jax.random.split(key, 5)
    order = jax.random.permutation(parts[0], ROWS)
    expert_order = jax.random.permutation(parts[1], FLIGHT)
    second_load = jax.random.randint(parts[2], (), ROWS // FLIGHT, CAP + 1)
    ranks = jnp.arange(ROWS)
    remaining = ranks - CAP - second_load
    which = jnp.where(ranks < CAP, 0, jnp.where(ranks < CAP + second_load, 1, 2 + remaining % (FLIGHT - 2)))
    slot_rank = jnp.where(ranks < CAP, ranks, jnp.where(ranks < CAP + second_load, ranks - CAP, remaining // (FLIGHT - 2)))
    expert_rank = expert_order[which]
    own = jnp.zeros((ROWS,), jnp.int32).at[order].set(expert_rank.astype(jnp.int32))
    slot_place = jnp.zeros((ROWS,), jnp.int32).at[order].set(slot_rank.astype(jnp.int32))
    position = jax.random.randint(parts[3], (ROWS,), 0, TOP)
    group_width = (EXPERTS - FLIGHT) // (TOP - 1)
    band = (jnp.arange(TOP)[None, :] - position[:, None]) % TOP
    offset = jax.random.randint(parts[4], (ROWS, TOP), 0, group_width)
    others = FLIGHT + (band - 1) * group_width + offset
    chosen = jnp.where(band == 0, own[:, None], others)
    return (chosen.astype(jnp.int32), slot_place)


def draw_routes(key, part):
    chosen, slot_place = routing_plan(key)
    return chosen


def draw_capacity_slot(key, part):
    chosen, slot_place = routing_plan(key)
    return slot_place


def draw_key_cache(key, part):
    base = shared_keys(key)
    return base.astype(jnp.bfloat16)


def draw_queries(key, part):
    key = jax.random.fold_in(key, 12)
    parts = jax.random.split(key, 1)
    values = jnp.clip(jax.random.normal(parts[0], (ROWS, QH, HD), jnp.float32), -4.5, 4.5)
    return values.astype(jnp.bfloat16)


def draw_lengths(key, part):
    key = jax.random.fold_in(key, 13)
    parts = jax.random.split(key, 2)
    drawn = jax.random.randint(parts[0], (ROWS,), 2, CACHE + 1)
    longest = jax.random.randint(parts[1], (), 0, ROWS)
    return jnp.where(jnp.arange(ROWS) == longest, CACHE, drawn).astype(jnp.int32)


def draw_router(key, part):
    key = jax.random.fold_in(key, 14)
    parts = jax.random.split(key, 1)
    values = jnp.clip(jax.random.normal(parts[0], (D, EXPERTS), jnp.float32), -4.5, 4.5) * (3.0 / math.sqrt(D))
    return values.astype(jnp.bfloat16)


def steps_of(key, extent, cuts, smallest, high):
    def one(dim, shards_of):
        heights = jax.random.uniform(jax.random.fold_in(jax.random.fold_in(key, 6), dim), (shards_of,), jnp.float32, smallest / len(cuts), high / len(cuts))
        return jnp.repeat(jnp.exp(heights), extent[dim] // shards_of).reshape((-1,) + (1,) * (len(extent) - dim - 1))

    factor_of = one(*cuts[0])
    for cut in cuts[1:]:
        factor_of = factor_of * one(*cut)
    return factor_of


def noise(own_key, extent, width, bound, pieces=(), kind=jnp.bfloat16):
    level = steps_of(own_key, extent, pieces, -0.22, 0.18) if pieces else 1.0
    values = jax.random.normal(own_key, extent, jnp.float32) * width * level
    return jnp.minimum(jnp.maximum(values, -bound), bound).astype(kind)


def setup_inputs(seed: int = 0, part: int = 0) -> dict:
    splits = jax.random.split(jax.random.key(seed), 16)
    part_splits = jax.random.split(jax.random.fold_in(splits[15], part), 16)
    return {
        "queries": draw_queries(jax.random.fold_in(jax.random.fold_in(splits[15], part), 71), part),
        "new_key": noise(part_splits[1], (ROWS, KVH, HD), 1.0, 4.5, ((0, 8), (1, 2))),
        "new_value": noise(part_splits[2], (ROWS, KVH, HD), 1.0, 4.5, ((0, 8), (1, 2))),
        "key_cache": draw_key_cache(jax.random.fold_in(jax.random.fold_in(splits[15], part), 71), part),
        "value_cache": noise(part_splits[4], (ROWS, CACHE, KVH, HD), 1.0, 4.5, ((0, 8), (2, 2))),
        "lengths": draw_lengths(jax.random.fold_in(jax.random.fold_in(splits[15], part), 71), part),
        "w_out": noise(splits[6], (QH * HD, D), (QH * HD) ** -0.5, 0.0625, ((0, 2), (1, 8))),
        "resid_cols": noise(part_splits[7], (ROWS, D), 1.0, 6.0, ((1, 8),)),
        "norm_gain": jnp.clip(1.0 + 0.1 * jax.random.normal(splits[8], (D,), jnp.float32), 0.5, 1.5),
        "router": draw_router(jax.random.fold_in(splits[15], 71), part),
        "routes": draw_routes(jax.random.fold_in(jax.random.fold_in(splits[15], part), 71), part),
        "capacity_slot": draw_capacity_slot(jax.random.fold_in(jax.random.fold_in(splits[15], part), 71), part),
        "w_gate": noise(splits[12], (FLIGHT, D, FF), D ** -0.5, 0.09375, ((0, 4), (1, 2), (2, 2))),
        "w_up": noise(splits[13], (FLIGHT, D, FF), D ** -0.5, 0.09375, ((0, 4), (1, 2), (2, 2))),
        "w_down": noise(splits[14], (FLIGHT, FF, D), FF ** -0.5, 0.15625, ((0, 4), (1, 2), (2, 2))),
    }


def rms_norm(hidden, gain):
    values = hidden.astype(jnp.float32)
    mean_square = lax.optimization_barrier(jnp.mean(values * values, axis=-1, keepdims=True))
    return (values * lax.rsqrt(mean_square + 1e-06) * gain).astype(jnp.bfloat16)

def reference(queries, new_key, new_value, key_cache, value_cache, lengths, w_out, resid_cols, norm_gain, router, routes, capacity_slot, w_gate, w_up, w_down):
    group_size = QH // KVH
    score_scale = HD ** (-0.5)
    query_block = queries.astype(jnp.float32).reshape(ROWS, KVH, group_size, HD)
    scores_cache = jnp.einsum('rkgd,rlkd->rkgl', query_block, key_cache.astype(jnp.float32)) * score_scale
    score_new = jnp.einsum('rkgd,rkd->rkg', query_block, new_key.astype(jnp.float32)) * score_scale
    valid_mask = jnp.arange(CACHE)[None, :] < lengths[:, None]
    scores_cache = jnp.where(valid_mask[:, None, None, :], scores_cache, -jnp.inf)
    highest = jnp.maximum(lax.optimization_barrier(jnp.max(scores_cache, axis=-1)), score_new)
    exp_cache = jnp.exp(scores_cache - highest[..., None])
    exp_new = jnp.exp(score_new - highest)
    denominator = lax.optimization_barrier(jnp.sum(exp_cache, axis=-1)) + exp_new
    probs_cache = (exp_cache / denominator[..., None]).astype(jnp.bfloat16)
    probs_new = (exp_new / denominator).astype(jnp.bfloat16)
    mixed = jnp.einsum('rkgl,rlkd->rkgd', probs_cache.astype(jnp.float32), value_cache.astype(jnp.float32))
    mixed = mixed + probs_new.astype(jnp.float32)[..., None] * new_value.astype(jnp.float32)[:, :, None, :]
    attn = mixed.astype(jnp.bfloat16).reshape(ROWS, QH * HD)
    attn_proj = jnp.dot(attn, w_out, preferred_element_type=jnp.float32)
    hidden = (resid_cols.astype(jnp.float32) + attn_proj).astype(jnp.bfloat16)
    normed = rms_norm(hidden, norm_gain)
    logits = jnp.dot(normed, router, preferred_element_type=jnp.float32)
    picked = routes[:, :, None] == jnp.arange(EXPERTS)[None, None, :]
    chosen_logits = lax.optimization_barrier(jnp.sum(jnp.where(picked, logits[:, None, :], 0.0), axis=-1))
    gate_prob = jax.nn.softmax(chosen_logits, axis=-1)
    own = lax.optimization_barrier(jnp.min(routes, axis=1)).astype(jnp.int32)
    share = lax.optimization_barrier(jnp.sum(jnp.where(routes == own[:, None], gate_prob, 0.0), axis=1))
    slot_range = jnp.arange(CAP)

    def one_expert(running, item):
        gate_weight, up_weight, down_weight, index = item
        is_mine = own == index
        dispatch = ((slot_range[:, None] == capacity_slot[None, :]) & is_mine[None, :]).astype(jnp.bfloat16)
        buffer = jnp.dot(dispatch, normed, preferred_element_type=jnp.float32).astype(jnp.bfloat16)
        expert_gate = jnp.dot(buffer, gate_weight, preferred_element_type=jnp.float32)
        expert_up = jnp.dot(buffer, up_weight, preferred_element_type=jnp.float32)
        activated = (jax.nn.silu(expert_gate) * expert_up).astype(jnp.bfloat16)
        expert_out = jnp.dot(activated, down_weight, preferred_element_type=jnp.float32)
        placed = jnp.take(expert_out, capacity_slot, axis=0)
        return (running + jnp.where(is_mine, share, 0.0)[:, None] * placed, None)
    start_total = jnp.zeros((ROWS, D), jnp.float32)
    indices = jnp.arange(FLIGHT, dtype=jnp.int32)
    routed, _ = lax.scan(one_expert, start_total, (w_gate, w_up, w_down, indices))
    return (hidden.astype(jnp.float32) + routed).astype(jnp.bfloat16)
```

```python
import functools

import jax
import jax.numpy as jnp
from jax import lax
from jax.experimental import pallas as pl
from jax.experimental.pallas import tpu as pltpu
from jax.sharding import PartitionSpec as P


def rms_norm(hidden, gain):
    values = hidden.astype(jnp.float32)
    mean_square = jnp.mean(values * values, axis=-1, keepdims=True)
    return (values * lax.rsqrt(mean_square + 1e-06) * gain).astype(jnp.bfloat16)


def plain_body(
    queries,
    new_key,
    new_value,
    key_cache,
    value_cache,
    lengths,
    w_out,
    resid_cols,
    norm_gain,
    router,
    routes,
    capacity_slot,
    w_gate,
    w_up,
    w_down,
):
    rows_dev, heads_dev, head_size = queries.shape
    cache_len = key_cache.shape[1]
    kv_dev = key_cache.shape[2]
    group_size = heads_dev // kv_dev
    score_scale = head_size ** (-0.5)
    query_block = queries.reshape(rows_dev, kv_dev, group_size, head_size)
    scores_cache = (
        jnp.einsum("rkgd,rlkd->rkgl", query_block, key_cache, preferred_element_type=jnp.float32)
        * score_scale
    )
    score_new = (
        jnp.einsum("rkgd,rkd->rkg", query_block, new_key, preferred_element_type=jnp.float32)
        * score_scale
    )
    valid_mask = jnp.arange(cache_len)[None, :] < lengths[:, None]
    scores_cache = jnp.where(valid_mask[:, None, None, :], scores_cache, -jnp.inf)
    highest = jnp.maximum(jnp.max(scores_cache, axis=-1), score_new)
    exp_cache = jnp.exp(scores_cache - highest[..., None])
    exp_new = jnp.exp(score_new - highest)
    denominator = jnp.sum(exp_cache, axis=-1) + exp_new
    probs_cache = (exp_cache / denominator[..., None]).astype(jnp.bfloat16)
    probs_new = (exp_new / denominator).astype(jnp.bfloat16)
    mixed = jnp.einsum(
        "rkgl,rlkd->rkgd", probs_cache, value_cache, preferred_element_type=jnp.float32
    )
    mixed = (
        mixed
        + probs_new.astype(jnp.float32)[..., None] * new_value.astype(jnp.float32)[:, :, None, :]
    )
    attn = mixed.astype(jnp.bfloat16).reshape(rows_dev, heads_dev * head_size)
    partial_proj = jnp.dot(
        lax.all_gather(attn, ("expert", "dp"), axis=0, tiled=True),
        w_out,
        preferred_element_type=jnp.float32,
    )
    attn_proj = lax.psum(partial_proj, "head")
    hidden_cols = (resid_cols.astype(jnp.float32) + attn_proj).astype(jnp.bfloat16)
    head_index = lax.axis_index("head")
    half_width = w_gate.shape[1]
    hidden_rows = lax.all_to_all(
        hidden_cols, ("expert", "dp"), split_axis=0, concat_axis=1, tiled=True
    )
    normed_own = rms_norm(hidden_rows, norm_gain)
    normed = lax.all_gather(normed_own, ("expert", "dp"), axis=0, tiled=True)
    hidden_own = lax.dynamic_slice_in_dim(hidden_rows, head_index * half_width, half_width, 1)
    all_rows = normed.shape[0]
    logits = jnp.dot(normed, router, preferred_element_type=jnp.float32)
    picked = routes[:, :, None] == jnp.arange(router.shape[1])[None, None, :]
    chosen_logits = jnp.sum(jnp.where(picked, logits[:, None, :], 0.0), axis=-1)
    gate_prob = jax.nn.softmax(chosen_logits, axis=-1)
    own = jnp.min(routes, axis=1)
    share = jnp.sum(jnp.where(routes == own[:, None], gate_prob, 0.0), axis=1)
    capacity = all_rows // 4
    expert_index = lax.axis_index("expert")
    is_mine = own == expert_index
    dispatch = (
        (jnp.arange(capacity)[:, None] == capacity_slot[None, :]) & is_mine[None, :]
    ).astype(jnp.bfloat16)
    buffer = jnp.dot(dispatch, normed, preferred_element_type=jnp.float32).astype(jnp.bfloat16)
    mine_half = lax.dynamic_slice_in_dim(buffer, head_index * half_width, half_width, 1)
    gate_local = w_gate[0]
    up_local = w_up[0]
    down_local = w_down[0]
    gate_part = jnp.dot(mine_half, gate_local, preferred_element_type=jnp.float32)
    up_part = jnp.dot(mine_half, up_local, preferred_element_type=jnp.float32)
    expert_gate, expert_up = lax.psum((gate_part, up_part), "head")
    activated = (jax.nn.silu(expert_gate) * expert_up).astype(jnp.bfloat16)
    expert_out = jnp.dot(activated, down_local, preferred_element_type=jnp.float32)
    row_share = jnp.where(is_mine, share, 0.0)
    routed = lax.psum_scatter(
        jnp.take(expert_out, capacity_slot, axis=0) * row_share[:, None],
        ("expert", "dp"),
        scatter_dimension=0,
        tiled=True,
    )
    return (hidden_own.astype(jnp.float32) + routed).astype(jnp.bfloat16)


MESH = pl.DeviceIdType.MESH
F32, BF16 = jnp.float32, jnp.bfloat16


def step_kernel(
    experts_axis,
    dp_axis,
    lengths,
    queries,
    new_key,
    new_value,
    keys,
    values,
    w_out,
    resid,
    gain,
    router,
    routes,
    w_gate,
    w_up,
    w_down,
    out,
    q_v,
    k_v,
    v_v,
    wo_v,
    res_v,
    gain_v,
    rt_v,
    routes_v,
    wg_v,
    wu_v,
    wd_v,
    attn_all,
    attn_f32,
    attn_mat,
    proj_mine,
    proj_other,
    hid_send,
    hid_all,
    sq_all,
    gate_mine,
    gate_other,
    up_mine,
    up_other,
    logit_mine,
    logit_other,
    y_send,
    y_recv,
    load_sem,
    attn_ssem,
    attn_rsem,
    hid_ssem,
    hid_rsem,
    sq_ssem,
    sq_rsem,
    pair_ssem,
    pair_rsem,
    y_ssem,
    y_rsem,
):
    blocks = experts_axis * dp_axis
    half_blocks = blocks // 2
    expert, dp, head = lax.axis_index("expert"), lax.axis_index("dp"), lax.axis_index("head")
    me = expert * dp_axis + dp
    rows_dev, heads_dev, head_size = queries.shape
    rows = rows_dev * blocks
    half_width = w_gate.shape[0]
    cols = w_out.shape[1]
    kv_dev = new_key.shape[1]
    group_size = heads_dev // kv_dev

    def device(block, head_index):
        return {
            "expert": lax.div(block, dp_axis),
            "dp": lax.rem(block, dp_axis),
            "head": head_index,
        }

    def peer(k):
        return lax.rem(me + k, blocks)

    barrier = pltpu.get_barrier_semaphore()
    for k in range(blocks):
        if k:
            pl.semaphore_signal(barrier, 1, device_id=device(peer(k), head), device_id_type=MESH)
        pl.semaphore_signal(barrier, 1, device_id=device(peer(k), 1 - head), device_id_type=MESH)

    half_start = pl.multiple_of(head * half_width, half_width)
    loads = [
        pltpu.make_async_copy(src, dst, load_sem.at[i])
        for i, (src, dst) in enumerate(
            (
                (queries, q_v),
                (keys, k_v),
                (values, v_v),
                (w_out, wo_v),
                (resid, res_v),
                (gain.at[:, pl.ds(half_start, half_width)], gain_v),
                (routes, routes_v),
                (router.at[pl.ds(half_start, half_width), :], rt_v),
                (w_gate, wg_v),
                (w_up, wu_v),
                (w_down, wd_v),
            )
        )
    ]
    for load in loads:
        load.start()
    (ld_q, ld_k, ld_v, ld_wo, ld_res, ld_gain, ld_routes, ld_rt, ld_wg, ld_wu, ld_wd) = loads

    cached = keys.shape[1]
    scale = head_size ** (-0.5)
    column = lax.broadcasted_iota(jnp.int32, (heads_dev, cached), 1)
    head_of = lax.broadcasted_iota(jnp.int32, (heads_dev, cached), 0)
    position = lax.div(column, kv_dev)
    same_kv = lax.rem(column, kv_dev) == lax.div(head_of, group_size)
    kv_of = lax.div(lax.broadcasted_iota(jnp.int32, (heads_dev, head_size), 0), group_size)
    ld_q.wait()
    ld_k.wait()
    ld_v.wait()
    for r in range(rows_dev):
        q = q_v[r]
        scores = (
            lax.dot_general(q, k_v[r], (((1,), (1,)), ((), ())), preferred_element_type=F32)
            * scale
        )
        fresh_key = jnp.zeros((heads_dev, head_size), F32)
        fresh_value = jnp.zeros((heads_dev, head_size), F32)
        for k in range(kv_dev):
            fresh_key = jnp.where(kv_of == k, new_key[r, k : k + 1, :].astype(F32), fresh_key)
            fresh_value = jnp.where(kv_of == k, new_value[r, k : k + 1, :].astype(F32), fresh_value)
        score_new = jnp.sum(q.astype(F32) * fresh_key, axis=-1, keepdims=True) * scale
        scores = jnp.where(same_kv & (position < lengths[r]), scores, -jnp.inf)
        highest = jnp.maximum(jnp.max(scores, axis=-1, keepdims=True), score_new)
        exp_cache = jnp.exp(scores - highest)
        exp_new = jnp.exp(score_new - highest)
        inverse = 1.0 / (jnp.sum(exp_cache, axis=-1, keepdims=True) + exp_new)
        probs = (exp_cache * inverse).astype(BF16)
        probs_new = (exp_new * inverse).astype(BF16).astype(F32)
        mixed = jnp.dot(probs, v_v[r], preferred_element_type=F32) + probs_new * fresh_value
        attn_all[me, r * heads_dev : (r + 1) * heads_dev, :] = mixed.astype(BF16)

    pl.semaphore_wait(barrier, 2 * blocks - 1)

    def exchange(buffer, ssem, rsem, k):
        to = peer(k)
        return pltpu.make_async_remote_copy(
            src_ref=buffer.at[me],
            dst_ref=buffer.at[me],
            send_sem=ssem.at[to],
            recv_sem=rsem.at[me],
            device_id=device(to, head),
            device_id_type=MESH,
        )

    def arrival(src, dst, ssem, rsem, block):
        return pltpu.make_async_remote_copy(
            src_ref=src,
            dst_ref=dst,
            send_sem=ssem.at[block],
            recv_sem=rsem.at[block],
            device_id=device(block, head),
            device_id_type=MESH,
        )

    def to_sibling(src, dst, i):
        return pltpu.make_async_remote_copy(
            src_ref=src,
            dst_ref=dst,
            send_sem=pair_ssem.at[i],
            recv_sem=pair_rsem.at[i],
            device_id=device(me, 1 - head),
            device_id_type=MESH,
        )

    sends = [exchange(attn_all, attn_ssem, attn_rsem, k) for k in range(1, blocks)]
    for copy in sends:
        copy.start()
    block_rows = rows_dev * heads_dev

    def widen(block):
        start = pl.multiple_of(block * block_rows, block_rows)
        attn_f32[pl.ds(start, block_rows), :] = attn_all[block].astype(F32)

    widen(me)

    ld_routes.wait()
    picks = routes_v[...]
    expert_ids = lax.broadcasted_iota(jnp.int32, (rows, router.shape[1]), 1)
    picked = expert_ids == picks[:, 0:1]
    for k in range(1, picks.shape[1]):
        picked = picked | (expert_ids == picks[:, k : k + 1])
    own = jnp.min(picks, axis=1, keepdims=True)
    is_mine = own == expert

    for k in range(1, blocks):
        block = peer(blocks - k)
        arrival(attn_all.at[block], attn_all.at[block], attn_ssem, attn_rsem, block).wait_recv()
        widen(block)
    for h in range(heads_dev):
        attn_mat[:, h * head_size : (h + 1) * head_size] = attn_f32[
            pl.ds(h, rows, stride=heads_dev), :
        ].astype(BF16)

    ld_wo.wait()
    proj_mine[...] = jnp.dot(attn_mat[...], wo_v[...], preferred_element_type=F32)
    proj_copy = to_sibling(proj_mine, proj_other, 0)
    proj_copy.start()
    ld_res.wait()
    ld_gain.wait()
    proj_copy.wait_recv()
    hidden = (res_v[...].astype(F32) + (proj_mine[...] + proj_other[...])).astype(BF16)
    hid_send[...] = hidden
    squares = hidden.astype(F32)
    squares = jnp.sum(squares * squares, axis=-1, keepdims=True)
    row_is_lane = lax.broadcasted_iota(jnp.int32, (rows, 128), 0) == lax.broadcasted_iota(
        jnp.int32, (rows, 128), 1
    )
    half_of = lax.div(me, half_blocks)
    slot = lax.rem(me, half_blocks)
    stays = head == half_of
    target_dp = lax.rem(dp + jnp.where(stays, 0, 1), dp_axis)

    def hid_copy(k):
        to = lax.rem(expert + k, experts_axis)
        return pltpu.make_async_remote_copy(
            src_ref=hid_send,
            dst_ref=hid_all.at[slot],
            send_sem=hid_ssem.at[k],
            recv_sem=hid_rsem.at[slot],
            device_id={"expert": to, "dp": target_dp, "head": half_of},
            device_id_type=MESH,
        )

    for k in range(1, experts_axis):
        hid_copy(k).start()

    @pl.when(jnp.logical_not(stays))
    def _():
        hid_copy(0).start()

    @pl.when(stays)
    def _():
        hid_all[slot] = hidden

    sq_all[me] = jnp.sum(jnp.where(row_is_lane, squares, 0.0), axis=0, keepdims=True)
    sq_sends = [exchange(sq_all, sq_ssem, sq_rsem, k) for k in range(1, blocks)]
    for copy in sq_sends:
        copy.start()
    total = sq_all[me]
    for k in range(1, blocks):
        block = peer(blocks - k)
        arrival(sq_all.at[block], sq_all.at[block], sq_ssem, sq_rsem, block).wait_recv()
        total = total + sq_all[block]
    total = jnp.sum(jnp.where(row_is_lane, total, 0.0), axis=1, keepdims=True)
    inverse_rms = lax.rsqrt(total / (2 * half_width) + 1e-06)
    for i in range(half_blocks):

        @pl.when(jnp.logical_not(stays & (slot == i)))
        def _():
            pltpu.make_async_remote_copy(
                src_ref=hid_send,
                dst_ref=hid_all.at[i],
                send_sem=hid_ssem.at[0],
                recv_sem=hid_rsem.at[i],
                device_id=device(me, 1 - head),
                device_id_type=MESH,
            ).wait_recv()

    row_index = lax.broadcasted_iota(jnp.int32, (rows, 1), 0)
    is_own_row = lax.div(row_index, rows_dev) == me
    kept, pieces = [], []
    for i in range(half_blocks):
        values_f32 = hid_all[i].astype(F32)
        kept.append(jnp.where(is_own_row, values_f32, 0.0))
        pieces.append(
            (values_f32 * inverse_rms * gain_v[:, i * cols : (i + 1) * cols]).astype(BF16)
        )
    normed = jnp.concatenate(pieces, axis=1)

    ld_wg.wait()
    gate_mine[...] = jnp.dot(normed, wg_v[...], preferred_element_type=F32)
    gate_copy = to_sibling(gate_mine, gate_other, 1)
    gate_copy.start()
    ld_rt.wait()
    logit_mine[...] = jnp.dot(normed, rt_v[...], preferred_element_type=F32)
    logit_copy = to_sibling(logit_mine, logit_other, 2)
    logit_copy.start()
    ld_wu.wait()
    up_mine[...] = jnp.dot(normed, wu_v[...], preferred_element_type=F32)
    up_copy = to_sibling(up_mine, up_other, 3)
    up_copy.start()

    logit_copy.wait_recv()
    logits = jnp.where(picked, logit_mine[...] + logit_other[...], -jnp.inf)
    weights = jnp.exp(logits - jnp.max(logits, axis=1, keepdims=True))
    share = jnp.sum(jnp.where(expert_ids == own, weights, 0.0), axis=1, keepdims=True) / jnp.sum(
        weights, axis=1, keepdims=True
    )
    row_share = jnp.where(is_mine, share, 0.0)
    gate_copy.wait_recv()
    gate = gate_mine[...] + gate_other[...]
    gate = gate / (1.0 + jnp.exp(-gate))
    ld_wd.wait()
    up_copy.wait_recv()
    activated = (gate * (up_mine[...] + up_other[...])).astype(BF16)
    routed = jnp.dot(activated, wd_v[...], preferred_element_type=F32) * row_share
    routed = routed + jnp.concatenate(kept, axis=1)
    for block in range(blocks):
        y_send[block] = routed[block * rows_dev : (block + 1) * rows_dev, :]

    y_sends = []
    for k in range(1, blocks):
        to = peer(k)
        y_sends.append(
            pltpu.make_async_remote_copy(
                src_ref=y_send.at[to],
                dst_ref=y_recv.at[me],
                send_sem=y_ssem.at[to],
                recv_sem=y_rsem.at[me],
                device_id=device(to, head),
                device_id_type=MESH,
            )
        )
    for copy in y_sends:
        copy.start()
    result = y_send[me]
    for k in range(1, blocks):
        block = peer(blocks - k)
        arrival(y_send.at[block], y_recv.at[block], y_ssem, y_rsem, block).wait_recv()
        result = result + y_recv[block]
    out[...] = result

    for copy in sends + sq_sends + y_sends + [proj_copy, gate_copy, logit_copy, up_copy]:
        copy.wait_send()
    for k in range(1, experts_axis):
        hid_copy(k).wait_send()

    @pl.when(jnp.logical_not(stays))
    def _():
        hid_copy(0).wait_send()


def body(
    experts_axis,
    dp_axis,
    queries,
    new_key,
    new_value,
    key_cache,
    value_cache,
    lengths,
    w_out,
    resid_cols,
    norm_gain,
    router,
    routes,
    capacity_slot,
    w_gate,
    w_up,
    w_down,
):
    blocks = experts_axis * dp_axis
    rows_dev, heads_dev, head_size = queries.shape
    cache_len, kv_dev = key_cache.shape[1:3]
    rows = rows_dev * blocks
    cols = w_out.shape[1]
    half_width, ff_dev = w_gate.shape[1:]
    names = router.shape[1]
    if cols % 128 or ff_dev % 128 or rows > 64 or rows % 16 or blocks % 2 or dp_axis != 2:
        return plain_body(
            queries,
            new_key,
            new_value,
            key_cache,
            value_cache,
            lengths,
            w_out,
            resid_cols,
            norm_gain,
            router,
            routes,
            capacity_slot,
            w_gate,
            w_up,
            w_down,
        )
    half_blocks = blocks // 2
    dma = pltpu.SemaphoreType.DMA
    any_spec = pl.BlockSpec(memory_space=pl.ANY)
    vmem_spec = pl.BlockSpec(memory_space=pltpu.VMEM)
    cached = cache_len * kv_dev
    scratch = [
        pltpu.VMEM((rows_dev, heads_dev, head_size), BF16),
        pltpu.VMEM((rows_dev, cached, head_size), BF16),
        pltpu.VMEM((rows_dev, cached, head_size), BF16),
        pltpu.VMEM(w_out.shape, BF16),
        pltpu.VMEM(resid_cols.shape, BF16),
        pltpu.VMEM((1, half_width), F32),
        pltpu.VMEM((half_width, names), BF16),
        pltpu.VMEM(routes.shape, jnp.int32),
        pltpu.VMEM((half_width, ff_dev), BF16),
        pltpu.VMEM((half_width, ff_dev), BF16),
        pltpu.VMEM((ff_dev, half_width), BF16),
        pltpu.VMEM((blocks, rows_dev * heads_dev, head_size), BF16),
        pltpu.VMEM((rows * heads_dev, head_size), F32),
        pltpu.VMEM((rows, heads_dev * head_size), BF16),
        pltpu.VMEM((rows, cols), F32),
        pltpu.VMEM((rows, cols), F32),
        pltpu.VMEM((rows, cols), BF16),
        pltpu.VMEM((half_blocks, rows, cols), BF16),
        pltpu.VMEM((blocks, 1, 128), F32),
        pltpu.VMEM((rows, ff_dev), F32),
        pltpu.VMEM((rows, ff_dev), F32),
        pltpu.VMEM((rows, ff_dev), F32),
        pltpu.VMEM((rows, ff_dev), F32),
        pltpu.VMEM((rows, names), F32),
        pltpu.VMEM((rows, names), F32),
        pltpu.VMEM((blocks, rows_dev, half_width), F32),
        pltpu.VMEM((blocks, rows_dev, half_width), F32),
        dma((11,)),
        dma((blocks,)),
        dma((blocks,)),
        dma((experts_axis,)),
        dma((half_blocks,)),
        dma((blocks,)),
        dma((blocks,)),
        dma((4,)),
        dma((4,)),
        dma((blocks,)),
        dma((blocks,)),
    ]
    out = pl.pallas_call(
        functools.partial(step_kernel, experts_axis, dp_axis),
        out_shape=jax.ShapeDtypeStruct((rows_dev, half_width), F32),
        in_specs=[pl.BlockSpec(memory_space=pltpu.SMEM), any_spec, vmem_spec, vmem_spec]
        + [any_spec] * 10,
        out_specs=vmem_spec,
        scratch_shapes=scratch,
        compiler_params=pltpu.CompilerParams(
            collective_id=0, has_side_effects=True, vmem_limit_bytes=60 * 1024 * 1024
        ),
    )(
        lengths,
        queries,
        new_key,
        new_value,
        key_cache.reshape(rows_dev, cached, head_size),
        value_cache.reshape(rows_dev, cached, head_size),
        w_out,
        resid_cols,
        norm_gain[None, :],
        router,
        routes,
        w_gate[0],
        w_up[0],
        w_down[0],
    )
    return out.astype(BF16)


def solution(mesh):
    in_specs = (
        P(("groups", "expert", "dp"), "head", None),
        P(("groups", "expert", "dp"), "head", None),
        P(("groups", "expert", "dp"), "head", None),
        P(("groups", "expert", "dp"), None, "head", None),
        P(("groups", "expert", "dp"), None, "head", None),
        P(("groups", "expert", "dp")),
        P("head", ("expert", "dp")),
        P("groups", ("expert", "dp")),
        P(),
        P(),
        P("groups", None),
        P("groups"),
        P("expert", "head", "dp"),
        P("expert", "head", "dp"),
        P("expert", "dp", "head"),
    )
    out_specs = P(("groups", "expert", "dp"), "head")
    return jax.shard_map(
        functools.partial(body, mesh.shape["expert"], mesh.shape["dp"]),
        mesh=mesh, in_specs=in_specs, out_specs=out_specs, check_vma=False)
```

```python
import functools

import jax
import jax.numpy as jnp
from jax import lax
from jax.experimental import pallas as pl
from jax.experimental.pallas import tpu as pltpu
from jax.sharding import PartitionSpec as P


def rms_norm(hidden, gain):
    values = hidden.astype(jnp.float32)
    mean_square = jnp.mean(values * values, axis=-1, keepdims=True)
    return (values * lax.rsqrt(mean_square + 1e-06) * gain).astype(jnp.bfloat16)


def plain_body(
    queries,
    new_key,
    new_value,
    key_cache,
    value_cache,
    lengths,
    w_out,
    resid_cols,
    norm_gain,
    router,
    routes,
    capacity_slot,
    w_gate,
    w_up,
    w_down,
):
    rows_dev, heads_dev, head_size = queries.shape
    cache_len = key_cache.shape[1]
    kv_dev = key_cache.shape[2]
    group_size = heads_dev // kv_dev
    score_scale = head_size ** (-0.5)
    query_block = queries.reshape(rows_dev, kv_dev, group_size, head_size)
    scores_cache = (
        jnp.einsum("rkgd,rlkd->rkgl", query_block, key_cache, preferred_element_type=jnp.float32)
        * score_scale
    )
    score_new = (
        jnp.einsum("rkgd,rkd->rkg", query_block, new_key, preferred_element_type=jnp.float32)
        * score_scale
    )
    valid_mask = jnp.arange(cache_len)[None, :] < lengths[:, None]
    scores_cache = jnp.where(valid_mask[:, None, None, :], scores_cache, -jnp.inf)
    highest = jnp.maximum(jnp.max(scores_cache, axis=-1), score_new)
    exp_cache = jnp.exp(scores_cache - highest[..., None])
    exp_new = jnp.exp(score_new - highest)
    denominator = jnp.sum(exp_cache, axis=-1) + exp_new
    probs_cache = (exp_cache / denominator[..., None]).astype(jnp.bfloat16)
    probs_new = (exp_new / denominator).astype(jnp.bfloat16)
    mixed = jnp.einsum(
        "rkgl,rlkd->rkgd", probs_cache, value_cache, preferred_element_type=jnp.float32
    )
    mixed = (
        mixed
        + probs_new.astype(jnp.float32)[..., None] * new_value.astype(jnp.float32)[:, :, None, :]
    )
    attn = mixed.astype(jnp.bfloat16).reshape(rows_dev, heads_dev * head_size)
    partial_proj = jnp.dot(
        lax.all_gather(attn, ("expert", "dp"), axis=0, tiled=True),
        w_out,
        preferred_element_type=jnp.float32,
    )
    attn_proj = lax.psum(partial_proj, "head")
    hidden_cols = (resid_cols.astype(jnp.float32) + attn_proj).astype(jnp.bfloat16)
    head_index = lax.axis_index("head")
    half_width = w_gate.shape[1]
    hidden_rows = lax.all_to_all(
        hidden_cols, ("expert", "dp"), split_axis=0, concat_axis=1, tiled=True
    )
    normed_own = rms_norm(hidden_rows, norm_gain)
    normed = lax.all_gather(normed_own, ("expert", "dp"), axis=0, tiled=True)
    hidden_own = lax.dynamic_slice_in_dim(hidden_rows, head_index * half_width, half_width, 1)
    all_rows = normed.shape[0]
    logits = jnp.dot(normed, router, preferred_element_type=jnp.float32)
    picked = routes[:, :, None] == jnp.arange(router.shape[1])[None, None, :]
    chosen_logits = jnp.sum(jnp.where(picked, logits[:, None, :], 0.0), axis=-1)
    gate_prob = jax.nn.softmax(chosen_logits, axis=-1)
    own = jnp.min(routes, axis=1)
    share = jnp.sum(jnp.where(routes == own[:, None], gate_prob, 0.0), axis=1)
    capacity = all_rows // 4
    expert_index = lax.axis_index("expert")
    is_mine = own == expert_index
    dispatch = (
        (jnp.arange(capacity)[:, None] == capacity_slot[None, :]) & is_mine[None, :]
    ).astype(jnp.bfloat16)
    buffer = jnp.dot(dispatch, normed, preferred_element_type=jnp.float32).astype(jnp.bfloat16)
    mine_half = lax.dynamic_slice_in_dim(buffer, head_index * half_width, half_width, 1)
    gate_local = w_gate[0]
    up_local = w_up[0]
    down_local = w_down[0]
    gate_part = jnp.dot(mine_half, gate_local, preferred_element_type=jnp.float32)
    up_part = jnp.dot(mine_half, up_local, preferred_element_type=jnp.float32)
    expert_gate, expert_up = lax.psum((gate_part, up_part), "head")
    activated = (jax.nn.silu(expert_gate) * expert_up).astype(jnp.bfloat16)
    expert_out = jnp.dot(activated, down_local, preferred_element_type=jnp.float32)
    row_share = jnp.where(is_mine, share, 0.0)
    routed = lax.psum_scatter(
        jnp.take(expert_out, capacity_slot, axis=0) * row_share[:, None],
        ("expert", "dp"),
        scatter_dimension=0,
        tiled=True,
    )
    return (hidden_own.astype(jnp.float32) + routed).astype(jnp.bfloat16)


MESH = pl.DeviceIdType.MESH
F32, BF16 = jnp.float32, jnp.bfloat16


def step_kernel(
    experts_axis,
    dp_axis,
    lengths,
    queries,
    new_key,
    new_value,
    keys,
    values,
    w_out,
    resid,
    gain,
    router,
    routes,
    w_gate,
    w_up,
    w_down,
    out,
    q_v,
    lengths_v,
    nk_v,
    nv_v,
    k_v,
    v_v,
    wo_v,
    res_v,
    gain_v,
    rt_v,
    routes_v,
    wg_v,
    wu_v,
    wd_v,
    attn_all,
    attn_f32,
    attn_mat,
    proj_mine,
    proj_other,
    hid_send,
    hid_all,
    sq_mine,
    sq_other,
    gate_mine,
    gate_other,
    up_mine,
    up_other,
    logit_mine,
    logit_other,
    y_mine,
    y_send,
    y_recv,
    load_sem,
    attn_ssem,
    attn_rsem,
    hid_ssem,
    hid_rsem,
    pair_ssem,
    pair_rsem,
    y_ssem,
    y_rsem,
):
    blocks = experts_axis * dp_axis
    half_blocks = blocks // 2
    expert, dp, head = lax.axis_index("expert"), lax.axis_index("dp"), lax.axis_index("head")
    me = expert * dp_axis + dp
    rows_dev, heads_dev, head_size = queries.shape
    rows = rows_dev * blocks
    half_width = w_gate.shape[0]
    cols = w_out.shape[1]
    kv_dev = new_key.shape[1]
    group_size = heads_dev // kv_dev

    def device(block, head_index):
        return {
            "expert": lax.div(block, dp_axis),
            "dp": lax.rem(block, dp_axis),
            "head": head_index,
        }

    def peer(k):
        other, rest, bit = 0, me, 1
        while bit < blocks:
            digit = lax.rem(rest, 2)
            other = other + bit * (1 - digit if k & bit else digit)
            rest, bit = lax.div(rest, 2), 2 * bit
        return other

    half_start = pl.multiple_of(head * half_width, half_width)
    loads = [
        pltpu.make_async_copy(src, dst, load_sem.at[i])
        for i, (src, dst) in enumerate(
            (
                (keys, k_v),
                (queries, q_v),
                (lengths, lengths_v),
                (new_key, nk_v),
                (new_value, nv_v),
                (values, v_v),
                (w_out, wo_v),
                (resid, res_v),
                (gain.at[:, pl.ds(half_start, half_width)], gain_v),
                (routes, routes_v),
                (router.at[pl.ds(half_start, half_width), :], rt_v),
                (w_gate, wg_v),
                (w_up, wu_v),
                (w_down, wd_v),
            )
        )
    ]
    for load in loads[:6]:
        load.start()

    barrier = pltpu.get_barrier_semaphore()
    for k in reversed(range(blocks)):
        if k:
            pl.semaphore_signal(barrier, 1, device_id=device(peer(k), head), device_id_type=MESH)
        pl.semaphore_signal(barrier, 1, device_id=device(peer(k), 1 - head), device_id_type=MESH)
    (ld_k, ld_q, ld_len, ld_nk, ld_nv, ld_v, ld_wo, ld_res, ld_gain, ld_routes, ld_rt, ld_wg, ld_wu, ld_wd) = loads

    cached = keys.shape[1]
    scale = head_size ** (-0.5)
    column = lax.broadcasted_iota(jnp.int32, (heads_dev, cached), 1)
    head_of = lax.broadcasted_iota(jnp.int32, (heads_dev, cached), 0)
    position = lax.div(column, kv_dev)
    same_kv = lax.rem(column, kv_dev) == lax.div(head_of, group_size)
    kv_of = lax.div(lax.broadcasted_iota(jnp.int32, (heads_dev, head_size), 0), group_size)
    ld_q.wait()
    ld_len.wait()
    ld_nk.wait()
    ld_nv.wait()
    ld_k.wait()
    ld_v.wait()
    for load in loads[6:]:
        load.start()
    for r in range(rows_dev):
        q = q_v[r]
        scores = (
            lax.dot_general(q, k_v[r], (((1,), (1,)), ((), ())), preferred_element_type=F32)
            * scale
        )
        fresh_key = jnp.zeros((heads_dev, head_size), F32)
        fresh_value = jnp.zeros((heads_dev, head_size), F32)
        for k in range(kv_dev):
            fresh_key = jnp.where(kv_of == k, nk_v[r, k : k + 1, :].astype(F32), fresh_key)
            fresh_value = jnp.where(kv_of == k, nv_v[r, k : k + 1, :].astype(F32), fresh_value)
        score_new = jnp.sum(q.astype(F32) * fresh_key, axis=-1, keepdims=True) * scale
        scores = jnp.where(same_kv & (position < lengths_v[r]), scores, -jnp.inf)
        highest = jnp.maximum(jnp.max(scores, axis=-1, keepdims=True), score_new)
        exp_cache = jnp.exp(scores - highest)
        exp_new = jnp.exp(score_new - highest)
        inverse = 1.0 / (jnp.sum(exp_cache, axis=-1, keepdims=True) + exp_new)
        probs = (exp_cache * inverse).astype(BF16)
        probs_new = (exp_new * inverse).astype(BF16).astype(F32)
        mixed = jnp.dot(probs, v_v[r], preferred_element_type=F32) + probs_new * fresh_value
        attn_all[me, r * heads_dev : (r + 1) * heads_dev, :] = mixed.astype(BF16)

    pl.semaphore_wait(barrier, 2 * blocks - 1)

    def exchange(buffer, ssem, rsem, k):
        to = peer(k)
        return pltpu.make_async_remote_copy(
            src_ref=buffer.at[me],
            dst_ref=buffer.at[me],
            send_sem=ssem.at[to],
            recv_sem=rsem.at[me],
            device_id=device(to, head),
            device_id_type=MESH,
        )

    def arrival(src, dst, ssem, rsem, block):
        return pltpu.make_async_remote_copy(
            src_ref=src,
            dst_ref=dst,
            send_sem=ssem.at[block],
            recv_sem=rsem.at[block],
            device_id=device(block, head),
            device_id_type=MESH,
        )

    def to_sibling(src, dst, i):
        return pltpu.make_async_remote_copy(
            src_ref=src,
            dst_ref=dst,
            send_sem=pair_ssem.at[i],
            recv_sem=pair_rsem.at[i],
            device_id=device(me, 1 - head),
            device_id_type=MESH,
        )

    sends = [exchange(attn_all, attn_ssem, attn_rsem, k) for k in reversed(range(1, blocks))]
    for copy in sends:
        copy.start()
    block_rows = rows_dev * heads_dev

    def widen(block):
        start = pl.multiple_of(block * block_rows, block_rows)
        attn_f32[pl.ds(start, block_rows), :] = attn_all[block].astype(F32)

    widen(me)

    ld_routes.wait()
    expert_ids = lax.broadcasted_iota(jnp.int32, (rows, router.shape[1]), 1)
    row_is_lane = lax.broadcasted_iota(jnp.int32, (rows, rows), 0) == lax.broadcasted_iota(
        jnp.int32, (rows, rows), 1
    )

    def pick(k):
        return jnp.sum(jnp.where(row_is_lane, routes_v[k : k + 1, :], 0), axis=1, keepdims=True)

    own = pick(0)
    picked = expert_ids == own
    for k in range(1, routes.shape[0]):
        chosen = pick(k)
        picked = picked | (expert_ids == chosen)
        own = jnp.minimum(own, chosen)
    is_mine = own == expert

    for k in range(1, blocks):
        block = peer(k)
        arrival(attn_all.at[block], attn_all.at[block], attn_ssem, attn_rsem, block).wait_recv()
        widen(block)
    for h in range(heads_dev):
        attn_mat[:, h * head_size : (h + 1) * head_size] = attn_f32[
            pl.ds(h, rows, stride=heads_dev), :
        ].astype(BF16)

    ld_wo.wait()
    proj_mine[...] = jnp.dot(attn_mat[...], wo_v[...], preferred_element_type=F32)
    proj_copy = to_sibling(proj_mine, proj_other, 0)
    proj_copy.start()
    ld_res.wait()
    ld_gain.wait()
    proj_copy.wait_recv()
    hidden = (res_v[...].astype(F32) + (proj_mine[...] + proj_other[...])).astype(BF16)
    hid_send[...] = hidden
    half_of = lax.div(me, half_blocks)
    slot = lax.rem(me, half_blocks)
    stays = head == half_of
    target_dp = lax.rem(dp + jnp.where(stays, 0, 1), dp_axis)

    def hid_copy(k):
        to = lax.div(peer(k * dp_axis), dp_axis)
        return pltpu.make_async_remote_copy(
            src_ref=hid_send,
            dst_ref=hid_all.at[slot],
            send_sem=hid_ssem.at[k],
            recv_sem=hid_rsem.at[slot],
            device_id={"expert": to, "dp": target_dp, "head": half_of},
            device_id_type=MESH,
        )

    for k in reversed(range(1, experts_axis)):
        hid_copy(k).start()

    @pl.when(jnp.logical_not(stays))
    def _():
        hid_copy(0).start()

    @pl.when(stays)
    def _():
        hid_all[slot] = hidden

    for copy in sends + [proj_copy]:
        copy.wait_send()

    for i in range(half_blocks):

        @pl.when(jnp.logical_not(stays & (slot == i)))
        def _():
            pltpu.make_async_remote_copy(
                src_ref=hid_send,
                dst_ref=hid_all.at[i],
                send_sem=hid_ssem.at[0],
                recv_sem=hid_rsem.at[i],
                device_id=device(me, 1 - head),
                device_id_type=MESH,
            ).wait_recv()

    lanes = sq_mine.shape[1]
    squares = jnp.zeros(sq_mine.shape, F32)
    blocks_f32 = [hid_all[i].astype(F32) for i in range(half_blocks)]
    for block in blocks_f32:
        for start in range(0, cols, lanes):
            part = block[:, start : start + lanes]
            squares = squares + part * part
    sq_mine[...] = squares
    sq_copy = to_sibling(sq_mine, sq_other, 4)
    sq_copy.start()
    row_index = lax.broadcasted_iota(jnp.int32, (rows, 1), 0)
    is_own_row = lax.div(row_index, rows_dev) == me
    kept = [jnp.where(is_own_row, block, 0.0) for block in blocks_f32]
    sq_copy.wait_recv()
    total = jnp.sum(sq_mine[...] + sq_other[...], axis=1, keepdims=True)
    inverse_rms = lax.rsqrt(total / (2 * half_width) + 1e-06)
    normed = jnp.concatenate(
        [
            (block * inverse_rms * gain_v[:, i * cols : (i + 1) * cols]).astype(BF16)
            for i, block in enumerate(blocks_f32)
        ],
        axis=1,
    )

    ld_wg.wait()
    gate_mine[...] = jnp.dot(normed, wg_v[...], preferred_element_type=F32)
    gate_copy = to_sibling(gate_mine, gate_other, 1)
    gate_copy.start()
    ld_rt.wait()
    logit_mine[...] = jnp.dot(normed, rt_v[...], preferred_element_type=F32)
    logit_copy = to_sibling(logit_mine, logit_other, 2)
    logit_copy.start()
    ld_wu.wait()
    up_mine[...] = jnp.dot(normed, wu_v[...], preferred_element_type=F32)
    up_copy = to_sibling(up_mine, up_other, 3)
    up_copy.start()

    sq_copy.wait_send()
    for k in range(1, experts_axis):
        hid_copy(k).wait_send()

    @pl.when(jnp.logical_not(stays))
    def _():
        hid_copy(0).wait_send()

    logit_copy.wait_recv()
    logits = jnp.where(picked, logit_mine[...] + logit_other[...], -jnp.inf)
    weights = jnp.exp(logits - jnp.max(logits, axis=1, keepdims=True))
    share = jnp.sum(jnp.where(expert_ids == own, weights, 0.0), axis=1, keepdims=True) / jnp.sum(
        weights, axis=1, keepdims=True
    )
    row_share = jnp.where(is_mine, share, 0.0)
    gate_copy.wait_recv()
    gate = gate_mine[...] + gate_other[...]
    gate = gate / (1.0 + jnp.exp(-gate))
    ld_wd.wait()
    up_copy.wait_recv()
    activated = (gate * (up_mine[...] + up_other[...])).astype(BF16)
    routed = jnp.dot(activated, wd_v[...], preferred_element_type=F32) * row_share
    routed = routed + jnp.concatenate(kept, axis=1)
    piece = y_mine.shape[2]
    for block in range(blocks):
        for i in range(half_width // piece):
            y_mine[block, i * rows_dev : (i + 1) * rows_dev, :] = routed[
                block * rows_dev : (block + 1) * rows_dev, i * piece : (i + 1) * piece
            ]
        y_send[block] = y_mine[block].astype(BF16)

    y_sends = []
    for k in reversed(range(1, blocks)):
        to = peer(k)
        y_sends.append(
            pltpu.make_async_remote_copy(
                src_ref=y_send.at[to],
                dst_ref=y_recv.at[me],
                send_sem=y_ssem.at[to],
                recv_sem=y_rsem.at[me],
                device_id=device(to, head),
                device_id_type=MESH,
            )
        )
    for copy in y_sends:
        copy.start()
    for copy in [gate_copy, logit_copy, up_copy] + y_sends:
        copy.wait_send()
    result = y_mine[me]
    for k in range(1, blocks):
        block = peer(k)
        arrival(y_send.at[block], y_recv.at[block], y_ssem, y_rsem, block).wait_recv()
        result = result + y_recv[block].astype(F32)
    for i in range(half_width // piece):
        out[:, i * piece : (i + 1) * piece] = result[i * rows_dev : (i + 1) * rows_dev, :]


def body(
    experts_axis,
    dp_axis,
    queries,
    new_key,
    new_value,
    key_cache,
    value_cache,
    lengths,
    w_out,
    resid_cols,
    norm_gain,
    router,
    routes,
    capacity_slot,
    w_gate,
    w_up,
    w_down,
):
    blocks = experts_axis * dp_axis
    rows_dev, heads_dev, head_size = queries.shape
    cache_len, kv_dev = key_cache.shape[1:3]
    rows = rows_dev * blocks
    cols = w_out.shape[1]
    half_width, ff_dev = w_gate.shape[1:]
    names = router.shape[1]
    if cols % 128 or ff_dev % 128 or rows > 64 or rows % 16 or blocks & (blocks - 1) or dp_axis != 2 or rows_dev != 2:
        return plain_body(
            queries,
            new_key,
            new_value,
            key_cache,
            value_cache,
            lengths,
            w_out,
            resid_cols,
            norm_gain,
            router,
            routes,
            capacity_slot,
            w_gate,
            w_up,
            w_down,
        )
    half_blocks = blocks // 2
    tile = 16
    dma = pltpu.SemaphoreType.DMA
    vmem_spec = pl.BlockSpec(memory_space=pltpu.VMEM)
    cached = cache_len * kv_dev
    scratch = [
        pltpu.VMEM((rows_dev, heads_dev, head_size), BF16),
        pltpu.SMEM((rows_dev,), jnp.int32),
        pltpu.VMEM(new_key.shape, BF16),
        pltpu.VMEM(new_value.shape, BF16),
        pltpu.VMEM((rows_dev, cached, head_size), BF16),
        pltpu.VMEM((rows_dev, cached, head_size), BF16),
        pltpu.VMEM(w_out.shape, BF16),
        pltpu.VMEM(resid_cols.shape, BF16),
        pltpu.VMEM((1, half_width), F32),
        pltpu.VMEM((half_width, names), BF16),
        pltpu.VMEM(routes.shape[::-1], jnp.int32),
        pltpu.VMEM((half_width, ff_dev), BF16),
        pltpu.VMEM((half_width, ff_dev), BF16),
        pltpu.VMEM((ff_dev, half_width), BF16),
        pltpu.VMEM((blocks, rows_dev * heads_dev, head_size), BF16),
        pltpu.VMEM((rows * heads_dev, head_size), F32),
        pltpu.VMEM((rows, heads_dev * head_size), BF16),
        pltpu.VMEM((rows, cols), F32),
        pltpu.VMEM((rows, cols), F32),
        pltpu.VMEM((rows, cols), BF16),
        pltpu.VMEM((half_blocks, rows, cols), BF16),
        pltpu.VMEM((rows, 128), F32),
        pltpu.VMEM((rows, 128), F32),
        pltpu.VMEM((rows, ff_dev), F32),
        pltpu.VMEM((rows, ff_dev), F32),
        pltpu.VMEM((rows, ff_dev), F32),
        pltpu.VMEM((rows, ff_dev), F32),
        pltpu.VMEM((rows, names), F32),
        pltpu.VMEM((rows, names), F32),
        pltpu.VMEM((blocks, tile, rows_dev * half_width // tile), F32),
        pltpu.VMEM((blocks, tile, rows_dev * half_width // tile), BF16),
        pltpu.VMEM((blocks, tile, rows_dev * half_width // tile), BF16),
        dma((14,)),
        dma((blocks,)),
        dma((blocks,)),
        dma((experts_axis,)),
        dma((half_blocks,)),
        dma((5,)),
        dma((5,)),
        dma((blocks,)),
        dma((blocks,)),
    ]
    out = pl.pallas_call(
        functools.partial(step_kernel, experts_axis, dp_axis),
        out_shape=pltpu.VMEM((rows_dev, half_width), F32),
        in_specs=[pl.BlockSpec(memory_space=pl.ANY)] * 14,
        out_specs=vmem_spec,
        scratch_shapes=scratch,
        compiler_params=pltpu.CompilerParams(
            collective_id=0, has_side_effects=True, vmem_limit_bytes=60 * 1024 * 1024
        ),
    )(
        lengths,
        queries,
        new_key,
        new_value,
        key_cache.reshape(rows_dev, cached, head_size),
        value_cache.reshape(rows_dev, cached, head_size),
        w_out,
        resid_cols,
        norm_gain[None, :],
        router,
        routes.T,
        w_gate[0],
        w_up[0],
        w_down[0],
    )
    return out.astype(BF16)


def solution(mesh):
    in_specs = (
        P(("groups", "expert", "dp"), "head", None),
        P(("groups", "expert", "dp"), "head", None),
        P(("groups", "expert", "dp"), "head", None),
        P(("groups", "expert", "dp"), None, "head", None),
        P(("groups", "expert", "dp"), None, "head", None),
        P(("groups", "expert", "dp")),
        P("head", ("expert", "dp")),
        P("groups", ("expert", "dp")),
        P(),
        P(),
        P("groups", None),
        P("groups"),
        P("expert", "head", "dp"),
        P("expert", "head", "dp"),
        P("expert", "dp", "head"),
    )
    out_specs = P(("groups", "expert", "dp"), "head")
    return jax.shard_map(
        functools.partial(body, mesh.shape["expert"], mesh.shape["dp"]),
        mesh=mesh, in_specs=in_specs, out_specs=out_specs, check_vma=False)
```

```python
import functools

import jax
import jax.numpy as jnp
from jax import lax
from jax.experimental import pallas as pl
from jax.experimental.pallas import tpu as pltpu
from jax.sharding import PartitionSpec as P


def rms_norm(hidden, gain):
    values = hidden.astype(jnp.float32)
    mean_square = jnp.mean(values * values, axis=-1, keepdims=True)
    return (values * lax.rsqrt(mean_square + 1e-06) * gain).astype(jnp.bfloat16)


def plain_body(
    queries,
    new_key,
    new_value,
    key_cache,
    value_cache,
    lengths,
    w_out,
    resid_cols,
    norm_gain,
    router,
    routes,
    capacity_slot,
    w_gate,
    w_up,
    w_down,
):
    rows_dev, heads_dev, head_size = queries.shape
    cache_len = key_cache.shape[1]
    kv_dev = key_cache.shape[2]
    group_size = heads_dev // kv_dev
    score_scale = head_size ** (-0.5)
    query_block = queries.reshape(rows_dev, kv_dev, group_size, head_size)
    scores_cache = (
        jnp.einsum("rkgd,rlkd->rkgl", query_block, key_cache, preferred_element_type=jnp.float32)
        * score_scale
    )
    score_new = (
        jnp.einsum("rkgd,rkd->rkg", query_block, new_key, preferred_element_type=jnp.float32)
        * score_scale
    )
    valid_mask = jnp.arange(cache_len)[None, :] < lengths[:, None]
    scores_cache = jnp.where(valid_mask[:, None, None, :], scores_cache, -jnp.inf)
    highest = jnp.maximum(jnp.max(scores_cache, axis=-1), score_new)
    exp_cache = jnp.exp(scores_cache - highest[..., None])
    exp_new = jnp.exp(score_new - highest)
    denominator = jnp.sum(exp_cache, axis=-1) + exp_new
    probs_cache = (exp_cache / denominator[..., None]).astype(jnp.bfloat16)
    probs_new = (exp_new / denominator).astype(jnp.bfloat16)
    mixed = jnp.einsum(
        "rkgl,rlkd->rkgd", probs_cache, value_cache, preferred_element_type=jnp.float32
    )
    mixed = (
        mixed
        + probs_new.astype(jnp.float32)[..., None] * new_value.astype(jnp.float32)[:, :, None, :]
    )
    attn = mixed.astype(jnp.bfloat16).reshape(rows_dev, heads_dev * head_size)
    partial_proj = jnp.dot(
        lax.all_gather(attn, ("expert", "dp"), axis=0, tiled=True),
        w_out,
        preferred_element_type=jnp.float32,
    )
    attn_proj = lax.psum(partial_proj, "head")
    hidden_cols = (resid_cols.astype(jnp.float32) + attn_proj).astype(jnp.bfloat16)
    head_index = lax.axis_index("head")
    half_width = w_gate.shape[1]
    hidden_rows = lax.all_to_all(
        hidden_cols, ("expert", "dp"), split_axis=0, concat_axis=1, tiled=True
    )
    normed_own = rms_norm(hidden_rows, norm_gain)
    normed = lax.all_gather(normed_own, ("expert", "dp"), axis=0, tiled=True)
    hidden_own = lax.dynamic_slice_in_dim(hidden_rows, head_index * half_width, half_width, 1)
    all_rows = normed.shape[0]
    logits = jnp.dot(normed, router, preferred_element_type=jnp.float32)
    picked = routes[:, :, None] == jnp.arange(router.shape[1])[None, None, :]
    chosen_logits = jnp.sum(jnp.where(picked, logits[:, None, :], 0.0), axis=-1)
    gate_prob = jax.nn.softmax(chosen_logits, axis=-1)
    own = jnp.min(routes, axis=1)
    share = jnp.sum(jnp.where(routes == own[:, None], gate_prob, 0.0), axis=1)
    capacity = all_rows // 4
    expert_index = lax.axis_index("expert")
    is_mine = own == expert_index
    dispatch = (
        (jnp.arange(capacity)[:, None] == capacity_slot[None, :]) & is_mine[None, :]
    ).astype(jnp.bfloat16)
    buffer = jnp.dot(dispatch, normed, preferred_element_type=jnp.float32).astype(jnp.bfloat16)
    mine_half = lax.dynamic_slice_in_dim(buffer, head_index * half_width, half_width, 1)
    gate_local = w_gate[0]
    up_local = w_up[0]
    down_local = w_down[0]
    gate_part = jnp.dot(mine_half, gate_local, preferred_element_type=jnp.float32)
    up_part = jnp.dot(mine_half, up_local, preferred_element_type=jnp.float32)
    expert_gate, expert_up = lax.psum((gate_part, up_part), "head")
    activated = (jax.nn.silu(expert_gate) * expert_up).astype(jnp.bfloat16)
    expert_out = jnp.dot(activated, down_local, preferred_element_type=jnp.float32)
    row_share = jnp.where(is_mine, share, 0.0)
    routed = lax.psum_scatter(
        jnp.take(expert_out, capacity_slot, axis=0) * row_share[:, None],
        ("expert", "dp"),
        scatter_dimension=0,
        tiled=True,
    )
    return (hidden_own.astype(jnp.float32) + routed).astype(jnp.bfloat16)


MESH = pl.DeviceIdType.MESH
F32, BF16 = jnp.float32, jnp.bfloat16


def step_kernel(
    experts_axis,
    dp_axis,
    lengths,
    queries,
    new_key,
    new_value,
    keys,
    values,
    w_out,
    resid,
    gain,
    router,
    routes,
    w_gate,
    w_up,
    w_down,
    out,
    q_v,
    lengths_v,
    nk_v,
    nv_v,
    k_v,
    v_v,
    wo_v,
    res_v,
    gain_v,
    rt_v,
    routes_v,
    wg_v,
    wu_v,
    wd_v,
    attn_all,
    attn_f32,
    attn_mat,
    proj_mine,
    proj_other,
    hid_send,
    hid_all,
    sq_mine,
    sq_all,
    gate_mine,
    gate_other,
    up_mine,
    up_other,
    logit_mine,
    logit_other,
    y_mine,
    y_send,
    y_recv,
    load_sem,
    attn_ssem,
    attn_rsem,
    hid_ssem,
    hid_rsem,
    sq_ssem,
    sq_rsem,
    pair_ssem,
    pair_rsem,
    y_ssem,
    y_rsem,
):
    blocks = experts_axis * dp_axis
    half_blocks = blocks // 2
    expert, dp, head = lax.axis_index("expert"), lax.axis_index("dp"), lax.axis_index("head")
    me = expert * dp_axis + dp
    rows_dev, heads_dev, head_size = queries.shape
    rows = rows_dev * blocks
    half_width = w_gate.shape[0]
    cols = w_out.shape[1]
    kv_dev = new_key.shape[1]
    group_size = heads_dev // kv_dev

    def device(block, head_index):
        return {
            "expert": lax.div(block, dp_axis),
            "dp": lax.rem(block, dp_axis),
            "head": head_index,
        }

    def peer(k):
        other, rest, bit = 0, me, 1
        while bit < blocks:
            digit = lax.rem(rest, 2)
            other = other + bit * (1 - digit if k & bit else digit)
            rest, bit = lax.div(rest, 2), 2 * bit
        return other

    barrier = pltpu.get_barrier_semaphore()
    for k in reversed(range(blocks)):
        if k:
            pl.semaphore_signal(barrier, 1, device_id=device(peer(k), head), device_id_type=MESH)
        pl.semaphore_signal(barrier, 1, device_id=device(peer(k), 1 - head), device_id_type=MESH)

    half_start = pl.multiple_of(head * half_width, half_width)
    loads = [
        pltpu.make_async_copy(src, dst, load_sem.at[i])
        for i, (src, dst) in enumerate(
            (
                (keys, k_v),
                (queries, q_v),
                (lengths, lengths_v),
                (new_key, nk_v),
                (new_value, nv_v),
                (values, v_v),
                (w_out, wo_v),
                (resid, res_v),
                (gain.at[:, pl.ds(half_start, half_width)], gain_v),
                (routes, routes_v),
                (router.at[pl.ds(half_start, half_width), :], rt_v),
                (w_gate, wg_v),
                (w_up, wu_v),
                (w_down, wd_v),
            )
        )
    ]
    for load in loads[:6]:
        load.start()
    (ld_k, ld_q, ld_len, ld_nk, ld_nv, ld_v, ld_wo, ld_res, ld_gain, ld_routes, ld_rt, ld_wg, ld_wu, ld_wd) = loads

    cached = keys.shape[1]
    scale = head_size ** (-0.5)
    column = lax.broadcasted_iota(jnp.int32, (heads_dev, cached), 1)
    head_of = lax.broadcasted_iota(jnp.int32, (heads_dev, cached), 0)
    position = lax.div(column, kv_dev)
    same_kv = lax.rem(column, kv_dev) == lax.div(head_of, group_size)
    kv_of = lax.div(lax.broadcasted_iota(jnp.int32, (heads_dev, head_size), 0), group_size)
    ld_q.wait()
    ld_len.wait()
    ld_nk.wait()
    ld_nv.wait()
    ld_k.wait()
    for load in loads[6:]:
        load.start()
    each = range(rows_dev)
    scores = [
        lax.dot_general(q_v[r], k_v[r], (((1,), (1,)), ((), ())), preferred_element_type=F32)
        for r in each
    ]
    fresh_keys, fresh_values = [], []
    for r in each:
        fresh_key = jnp.zeros((heads_dev, head_size), F32)
        fresh_value = jnp.zeros((heads_dev, head_size), F32)
        for k in range(kv_dev):
            fresh_key = jnp.where(kv_of == k, nk_v[r, k : k + 1, :].astype(F32), fresh_key)
            fresh_value = jnp.where(kv_of == k, nv_v[r, k : k + 1, :].astype(F32), fresh_value)
        fresh_keys.append(fresh_key)
        fresh_values.append(fresh_value)
    score_new = [
        jnp.sum(q_v[r].astype(F32) * fresh_keys[r], axis=-1, keepdims=True) * scale for r in each
    ]
    scores = [
        jnp.where(same_kv & (position < lengths_v[r]), scores[r] * scale, -jnp.inf) for r in each
    ]
    highest = [
        jnp.maximum(jnp.max(scores[r], axis=-1, keepdims=True), score_new[r]) for r in each
    ]
    exp_cache = [jnp.exp(scores[r] - highest[r]) for r in each]
    exp_new = [jnp.exp(score_new[r] - highest[r]) for r in each]
    inverse = [
        1.0 / (jnp.sum(exp_cache[r], axis=-1, keepdims=True) + exp_new[r]) for r in each
    ]
    probs = [(exp_cache[r] * inverse[r]).astype(BF16) for r in each]
    probs_new = [(exp_new[r] * inverse[r]).astype(BF16).astype(F32) for r in each]
    ld_v.wait()
    mixed = [jnp.dot(probs[r], v_v[r], preferred_element_type=F32) for r in each]
    for r in each:
        attn = mixed[r] + probs_new[r] * fresh_values[r]
        attn_all[me, r * heads_dev : (r + 1) * heads_dev, :] = attn.astype(BF16)

    pl.semaphore_wait(barrier, 2 * blocks - 1)

    def exchange(buffer, ssem, rsem, k):
        to = peer(k)
        return pltpu.make_async_remote_copy(
            src_ref=buffer.at[me],
            dst_ref=buffer.at[me],
            send_sem=ssem.at[to],
            recv_sem=rsem.at[me],
            device_id=device(to, head),
            device_id_type=MESH,
        )

    def arrival(src, dst, ssem, rsem, block):
        return pltpu.make_async_remote_copy(
            src_ref=src,
            dst_ref=dst,
            send_sem=ssem.at[block],
            recv_sem=rsem.at[block],
            device_id=device(block, head),
            device_id_type=MESH,
        )

    def to_sibling(src, dst, i):
        return pltpu.make_async_remote_copy(
            src_ref=src,
            dst_ref=dst,
            send_sem=pair_ssem.at[i],
            recv_sem=pair_rsem.at[i],
            device_id=device(me, 1 - head),
            device_id_type=MESH,
        )

    sends = [exchange(attn_all, attn_ssem, attn_rsem, k) for k in reversed(range(1, blocks))]
    for copy in sends:
        copy.start()
    block_rows = rows_dev * heads_dev

    def widen(block):
        start = pl.multiple_of(block * block_rows, block_rows)
        attn_f32[pl.ds(start, block_rows), :] = attn_all[block].astype(F32)

    widen(me)

    ld_routes.wait()
    expert_ids = lax.broadcasted_iota(jnp.int32, (rows, router.shape[1]), 1)
    row_is_lane = lax.broadcasted_iota(jnp.int32, (rows, rows), 0) == lax.broadcasted_iota(
        jnp.int32, (rows, rows), 1
    )

    def pick(k):
        return jnp.sum(jnp.where(row_is_lane, routes_v[k : k + 1, :], 0), axis=1, keepdims=True)

    own = pick(0)
    picked = expert_ids == own
    for k in range(1, routes.shape[0]):
        chosen = pick(k)
        picked = picked | (expert_ids == chosen)
        own = jnp.minimum(own, chosen)
    is_mine = own == expert

    for k in range(1, blocks):
        block = peer(k)
        arrival(attn_all.at[block], attn_all.at[block], attn_ssem, attn_rsem, block).wait_recv()
        widen(block)
    for h in range(heads_dev):
        attn_mat[:, h * head_size : (h + 1) * head_size] = attn_f32[
            pl.ds(h, rows, stride=heads_dev), :
        ].astype(BF16)

    ld_wo.wait()
    proj_mine[...] = jnp.dot(attn_mat[...], wo_v[...], preferred_element_type=F32)
    proj_copy = to_sibling(proj_mine, proj_other, 0)
    proj_copy.start()
    ld_res.wait()
    ld_gain.wait()
    proj_copy.wait_recv()
    hidden = (res_v[...].astype(F32) + (proj_mine[...] + proj_other[...])).astype(BF16)
    hid_send[...] = hidden
    half_of = lax.div(me, half_blocks)
    slot = lax.rem(me, half_blocks)
    stays = head == half_of
    target_dp = lax.rem(dp + jnp.where(stays, 0, 1), dp_axis)

    def hid_copy(k):
        to = lax.div(peer(k * dp_axis), dp_axis)
        return pltpu.make_async_remote_copy(
            src_ref=hid_send,
            dst_ref=hid_all.at[slot],
            send_sem=hid_ssem.at[k],
            recv_sem=hid_rsem.at[slot],
            device_id={"expert": to, "dp": target_dp, "head": half_of},
            device_id_type=MESH,
        )

    sq_dp = lax.rem(dp + jnp.where(stays, 1, 0), dp_axis)

    def sq_copy(k):
        to = lax.div(peer(k * dp_axis), dp_axis)
        return pltpu.make_async_remote_copy(
            src_ref=sq_mine,
            dst_ref=sq_all.at[slot],
            send_sem=sq_ssem.at[k],
            recv_sem=sq_rsem.at[slot],
            device_id={"expert": to, "dp": sq_dp, "head": 1 - half_of},
            device_id_type=MESH,
        )

    def lane_squares(block, total):
        for start in range(0, cols, total.shape[1]):
            part = block[:, start : start + total.shape[1]]
            total = total + part * part
        return total

    for k in reversed(range(1, experts_axis)):
        hid_copy(k).start()

    @pl.when(jnp.logical_not(stays))
    def _():
        hid_copy(0).start()

    own_squares = lane_squares(hidden.astype(F32), jnp.zeros(sq_mine.shape, F32))
    sq_mine[...] = own_squares
    for k in reversed(range(1, experts_axis)):
        sq_copy(k).start()

    @pl.when(stays)
    def _():
        sq_copy(0).start()
        hid_all[slot] = hidden

    @pl.when(jnp.logical_not(stays))
    def _():
        sq_all[slot] = own_squares

    for copy in sends + [proj_copy]:
        copy.wait_send()

    for i in range(half_blocks):

        @pl.when(jnp.logical_not(stays & (slot == i)))
        def _():
            pltpu.make_async_remote_copy(
                src_ref=hid_send,
                dst_ref=hid_all.at[i],
                send_sem=hid_ssem.at[0],
                recv_sem=hid_rsem.at[i],
                device_id=device(me, 1 - head),
                device_id_type=MESH,
            ).wait_recv()

    squares = jnp.zeros(sq_mine.shape, F32)
    blocks_f32 = [hid_all[i].astype(F32) for i in range(half_blocks)]
    for block in blocks_f32:
        squares = lane_squares(block, squares)
    for i in range(half_blocks):

        @pl.when(stays | (slot != i))
        def _():
            pltpu.make_async_remote_copy(
                src_ref=sq_mine,
                dst_ref=sq_all.at[i],
                send_sem=sq_ssem.at[0],
                recv_sem=sq_rsem.at[i],
                device_id=device(me, 1 - head),
                device_id_type=MESH,
            ).wait_recv()

        squares = squares + sq_all[i]
    row_index = lax.broadcasted_iota(jnp.int32, (rows, 1), 0)
    is_own_row = lax.div(row_index, rows_dev) == me
    kept = [jnp.where(is_own_row, block, 0.0) for block in blocks_f32]
    total = jnp.sum(squares, axis=1, keepdims=True)
    inverse_rms = lax.rsqrt(total / (2 * half_width) + 1e-06)
    normed = jnp.concatenate(
        [
            (block * inverse_rms * gain_v[:, i * cols : (i + 1) * cols]).astype(BF16)
            for i, block in enumerate(blocks_f32)
        ],
        axis=1,
    )

    ld_wg.wait()
    gate_mine[...] = jnp.dot(normed, wg_v[...], preferred_element_type=F32)
    gate_copy = to_sibling(gate_mine, gate_other, 1)
    gate_copy.start()
    ld_rt.wait()
    logit_mine[...] = jnp.dot(normed, rt_v[...], preferred_element_type=F32)
    logit_copy = to_sibling(logit_mine, logit_other, 2)
    logit_copy.start()
    ld_wu.wait()
    up_mine[...] = jnp.dot(normed, wu_v[...], preferred_element_type=F32)
    up_copy = to_sibling(up_mine, up_other, 3)
    up_copy.start()

    for k in range(1, experts_axis):
        hid_copy(k).wait_send()
        sq_copy(k).wait_send()

    @pl.when(stays)
    def _():
        sq_copy(0).wait_send()

    @pl.when(jnp.logical_not(stays))
    def _():
        hid_copy(0).wait_send()

    logit_copy.wait_recv()
    logits = jnp.where(picked, logit_mine[...] + logit_other[...], -jnp.inf)
    weights = jnp.exp(logits - jnp.max(logits, axis=1, keepdims=True))
    share = jnp.sum(jnp.where(expert_ids == own, weights, 0.0), axis=1, keepdims=True) / jnp.sum(
        weights, axis=1, keepdims=True
    )
    row_share = jnp.where(is_mine, share, 0.0)
    gate_copy.wait_recv()
    gate = gate_mine[...] + gate_other[...]
    gate = gate / (1.0 + jnp.exp(-gate))
    ld_wd.wait()
    up_copy.wait_recv()
    activated = (gate * (up_mine[...] + up_other[...])).astype(BF16)
    routed = jnp.dot(activated, wd_v[...], preferred_element_type=F32) * row_share
    routed = routed + jnp.concatenate(kept, axis=1)
    piece = y_mine.shape[2]
    for block in range(blocks):
        for i in range(half_width // piece):
            y_mine[block, i * rows_dev : (i + 1) * rows_dev, :] = routed[
                block * rows_dev : (block + 1) * rows_dev, i * piece : (i + 1) * piece
            ]
        y_send[block] = y_mine[block].astype(BF16)

    y_sends = []
    for k in reversed(range(1, blocks)):
        to = peer(k)
        y_sends.append(
            pltpu.make_async_remote_copy(
                src_ref=y_send.at[to],
                dst_ref=y_recv.at[me],
                send_sem=y_ssem.at[to],
                recv_sem=y_rsem.at[me],
                device_id=device(to, head),
                device_id_type=MESH,
            )
        )
    for copy in y_sends:
        copy.start()
    result = y_mine[me]
    for k in range(1, blocks):
        block = peer(k)
        arrival(y_send.at[block], y_recv.at[block], y_ssem, y_rsem, block).wait_recv()
        result = result + y_recv[block].astype(F32)
    for i in range(half_width // piece):
        out[:, i * piece : (i + 1) * piece] = result[i * rows_dev : (i + 1) * rows_dev, :]
    for copy in [gate_copy, logit_copy, up_copy] + y_sends:
        copy.wait_send()


def body(
    experts_axis,
    dp_axis,
    queries,
    new_key,
    new_value,
    key_cache,
    value_cache,
    lengths,
    w_out,
    resid_cols,
    norm_gain,
    router,
    routes,
    capacity_slot,
    w_gate,
    w_up,
    w_down,
):
    blocks = experts_axis * dp_axis
    rows_dev, heads_dev, head_size = queries.shape
    cache_len, kv_dev = key_cache.shape[1:3]
    rows = rows_dev * blocks
    cols = w_out.shape[1]
    half_width, ff_dev = w_gate.shape[1:]
    names = router.shape[1]
    if cols % 128 or ff_dev % 128 or rows > 64 or rows % 16 or blocks & (blocks - 1) or dp_axis != 2 or rows_dev != 2:
        return plain_body(
            queries,
            new_key,
            new_value,
            key_cache,
            value_cache,
            lengths,
            w_out,
            resid_cols,
            norm_gain,
            router,
            routes,
            capacity_slot,
            w_gate,
            w_up,
            w_down,
        )
    half_blocks = blocks // 2
    tile = 16
    dma = pltpu.SemaphoreType.DMA
    vmem_spec = pl.BlockSpec(memory_space=pltpu.VMEM)
    cached = cache_len * kv_dev
    scratch = [
        pltpu.VMEM((rows_dev, heads_dev, head_size), BF16),
        pltpu.SMEM((rows_dev,), jnp.int32),
        pltpu.VMEM(new_key.shape, BF16),
        pltpu.VMEM(new_value.shape, BF16),
        pltpu.VMEM((rows_dev, cached, head_size), BF16),
        pltpu.VMEM((rows_dev, cached, head_size), BF16),
        pltpu.VMEM(w_out.shape, BF16),
        pltpu.VMEM(resid_cols.shape, BF16),
        pltpu.VMEM((1, half_width), F32),
        pltpu.VMEM((half_width, names), BF16),
        pltpu.VMEM(routes.shape[::-1], jnp.int32),
        pltpu.VMEM((half_width, ff_dev), BF16),
        pltpu.VMEM((half_width, ff_dev), BF16),
        pltpu.VMEM((ff_dev, half_width), BF16),
        pltpu.VMEM((blocks, rows_dev * heads_dev, head_size), BF16),
        pltpu.VMEM((rows * heads_dev, head_size), F32),
        pltpu.VMEM((rows, heads_dev * head_size), BF16),
        pltpu.VMEM((rows, cols), F32),
        pltpu.VMEM((rows, cols), F32),
        pltpu.VMEM((rows, cols), BF16),
        pltpu.VMEM((half_blocks, rows, cols), BF16),
        pltpu.VMEM((rows, 128), F32),
        pltpu.VMEM((half_blocks, rows, 128), F32),
        pltpu.VMEM((rows, ff_dev), F32),
        pltpu.VMEM((rows, ff_dev), F32),
        pltpu.VMEM((rows, ff_dev), F32),
        pltpu.VMEM((rows, ff_dev), F32),
        pltpu.VMEM((rows, names), F32),
        pltpu.VMEM((rows, names), F32),
        pltpu.VMEM((blocks, tile, rows_dev * half_width // tile), F32),
        pltpu.VMEM((blocks, tile, rows_dev * half_width // tile), BF16),
        pltpu.VMEM((blocks, tile, rows_dev * half_width // tile), BF16),
        dma((14,)),
        dma((blocks,)),
        dma((blocks,)),
        dma((experts_axis,)),
        dma((half_blocks,)),
        dma((experts_axis,)),
        dma((half_blocks,)),
        dma((4,)),
        dma((4,)),
        dma((blocks,)),
        dma((blocks,)),
    ]
    out = pl.pallas_call(
        functools.partial(step_kernel, experts_axis, dp_axis),
        out_shape=pltpu.VMEM((rows_dev, half_width), F32),
        in_specs=[pl.BlockSpec(memory_space=pl.ANY)] * 14,
        out_specs=vmem_spec,
        scratch_shapes=scratch,
        compiler_params=pltpu.CompilerParams(
            collective_id=0, has_side_effects=True, vmem_limit_bytes=60 * 1024 * 1024
        ),
    )(
        lengths,
        queries,
        new_key,
        new_value,
        key_cache.reshape(rows_dev, cached, head_size),
        value_cache.reshape(rows_dev, cached, head_size),
        w_out,
        resid_cols,
        norm_gain[None, :],
        router,
        routes.T,
        w_gate[0],
        w_up[0],
        w_down[0],
    )
    return out.astype(BF16)


def solution(mesh):
    in_specs = (
        P(("groups", "expert", "dp"), "head", None),
        P(("groups", "expert", "dp"), "head", None),
        P(("groups", "expert", "dp"), "head", None),
        P(("groups", "expert", "dp"), None, "head", None),
        P(("groups", "expert", "dp"), None, "head", None),
        P(("groups", "expert", "dp")),
        P("head", ("expert", "dp")),
        P("groups", ("expert", "dp")),
        P(),
        P(),
        P("groups", None),
        P("groups"),
        P("expert", "head", "dp"),
        P("expert", "head", "dp"),
        P("expert", "dp", "head"),
    )
    out_specs = P(("groups", "expert", "dp"), "head")
    return jax.shard_map(
        functools.partial(body, mesh.shape["expert"], mesh.shape["dp"]),
        mesh=mesh, in_specs=in_specs, out_specs=out_specs, check_vma=False)
```

```python
import functools

import jax
import jax.numpy as jnp
from jax import lax
from jax.experimental import pallas as pl
from jax.experimental.pallas import tpu as pltpu
from jax.sharding import PartitionSpec as P


def rms_norm(hidden, gain):
    values = hidden.astype(jnp.float32)
    mean_square = jnp.mean(values * values, axis=-1, keepdims=True)
    return (values * lax.rsqrt(mean_square + 1e-06) * gain).astype(jnp.bfloat16)


def plain_body(
    queries,
    new_key,
    new_value,
    key_cache,
    value_cache,
    lengths,
    w_out,
    resid_cols,
    norm_gain,
    router,
    routes,
    capacity_slot,
    w_gate,
    w_up,
    w_down,
):
    rows_dev, heads_dev, head_size = queries.shape
    cache_len = key_cache.shape[1]
    kv_dev = key_cache.shape[2]
    group_size = heads_dev // kv_dev
    score_scale = head_size ** (-0.5)
    query_block = queries.reshape(rows_dev, kv_dev, group_size, head_size)
    scores_cache = (
        jnp.einsum("rkgd,rlkd->rkgl", query_block, key_cache, preferred_element_type=jnp.float32)
        * score_scale
    )
    score_new = (
        jnp.einsum("rkgd,rkd->rkg", query_block, new_key, preferred_element_type=jnp.float32)
        * score_scale
    )
    valid_mask = jnp.arange(cache_len)[None, :] < lengths[:, None]
    scores_cache = jnp.where(valid_mask[:, None, None, :], scores_cache, -jnp.inf)
    highest = jnp.maximum(jnp.max(scores_cache, axis=-1), score_new)
    exp_cache = jnp.exp(scores_cache - highest[..., None])
    exp_new = jnp.exp(score_new - highest)
    denominator = jnp.sum(exp_cache, axis=-1) + exp_new
    probs_cache = (exp_cache / denominator[..., None]).astype(jnp.bfloat16)
    probs_new = (exp_new / denominator).astype(jnp.bfloat16)
    mixed = jnp.einsum(
        "rkgl,rlkd->rkgd", probs_cache, value_cache, preferred_element_type=jnp.float32
    )
    mixed = (
        mixed
        + probs_new.astype(jnp.float32)[..., None] * new_value.astype(jnp.float32)[:, :, None, :]
    )
    attn = mixed.astype(jnp.bfloat16).reshape(rows_dev, heads_dev * head_size)
    partial_proj = jnp.dot(
        lax.all_gather(attn, ("expert", "dp"), axis=0, tiled=True),
        w_out,
        preferred_element_type=jnp.float32,
    )
    attn_proj = lax.psum(partial_proj, "head")
    hidden_cols = (resid_cols.astype(jnp.float32) + attn_proj).astype(jnp.bfloat16)
    head_index = lax.axis_index("head")
    half_width = w_gate.shape[1]
    hidden_rows = lax.all_to_all(
        hidden_cols, ("expert", "dp"), split_axis=0, concat_axis=1, tiled=True
    )
    normed_own = rms_norm(hidden_rows, norm_gain)
    normed = lax.all_gather(normed_own, ("expert", "dp"), axis=0, tiled=True)
    hidden_own = lax.dynamic_slice_in_dim(hidden_rows, head_index * half_width, half_width, 1)
    all_rows = normed.shape[0]
    logits = jnp.dot(normed, router, preferred_element_type=jnp.float32)
    picked = routes[:, :, None] == jnp.arange(router.shape[1])[None, None, :]
    chosen_logits = jnp.sum(jnp.where(picked, logits[:, None, :], 0.0), axis=-1)
    gate_prob = jax.nn.softmax(chosen_logits, axis=-1)
    own = jnp.min(routes, axis=1)
    share = jnp.sum(jnp.where(routes == own[:, None], gate_prob, 0.0), axis=1)
    capacity = all_rows // 4
    expert_index = lax.axis_index("expert")
    is_mine = own == expert_index
    dispatch = (
        (jnp.arange(capacity)[:, None] == capacity_slot[None, :]) & is_mine[None, :]
    ).astype(jnp.bfloat16)
    buffer = jnp.dot(dispatch, normed, preferred_element_type=jnp.float32).astype(jnp.bfloat16)
    mine_half = lax.dynamic_slice_in_dim(buffer, head_index * half_width, half_width, 1)
    gate_local = w_gate[0]
    up_local = w_up[0]
    down_local = w_down[0]
    gate_part = jnp.dot(mine_half, gate_local, preferred_element_type=jnp.float32)
    up_part = jnp.dot(mine_half, up_local, preferred_element_type=jnp.float32)
    expert_gate, expert_up = lax.psum((gate_part, up_part), "head")
    activated = (jax.nn.silu(expert_gate) * expert_up).astype(jnp.bfloat16)
    expert_out = jnp.dot(activated, down_local, preferred_element_type=jnp.float32)
    row_share = jnp.where(is_mine, share, 0.0)
    routed = lax.psum_scatter(
        jnp.take(expert_out, capacity_slot, axis=0) * row_share[:, None],
        ("expert", "dp"),
        scatter_dimension=0,
        tiled=True,
    )
    return (hidden_own.astype(jnp.float32) + routed).astype(jnp.bfloat16)


MESH = pl.DeviceIdType.MESH
F32, BF16 = jnp.float32, jnp.bfloat16


def step_kernel(
    experts_axis,
    dp_axis,
    lengths,
    queries,
    new_key,
    new_value,
    keys,
    values,
    w_out,
    resid,
    gain,
    router,
    routes,
    w_gate,
    w_up,
    w_down,
    out,
    q_v,
    lengths_v,
    nk_v,
    nv_v,
    k_v,
    v_v,
    wo_v,
    res_v,
    gain_v,
    rt_v,
    routes_v,
    wg_v,
    wu_v,
    wd_v,
    attn_all,
    attn_f32,
    attn_mat,
    proj_mine,
    proj_other,
    hid_send,
    hid_all,
    sq_mine,
    sq_all,
    gate_mine,
    gate_other,
    up_mine,
    up_other,
    logit_mine,
    logit_other,
    y_mine,
    y_send,
    y_recv,
    load_sem,
    attn_ssem,
    attn_rsem,
    hid_ssem,
    hid_rsem,
    sq_ssem,
    sq_rsem,
    pair_ssem,
    pair_rsem,
    y_ssem,
    y_rsem,
):
    blocks = experts_axis * dp_axis
    half_blocks = blocks // 2
    expert, dp, head = lax.axis_index("expert"), lax.axis_index("dp"), lax.axis_index("head")
    me = expert * dp_axis + dp
    rows_dev, heads_dev, head_size = queries.shape
    rows = rows_dev * blocks
    half_width = w_gate.shape[0]
    cols = w_out.shape[1]
    kv_dev = new_key.shape[1]
    group_size = heads_dev // kv_dev

    def device(block, head_index):
        return {
            "expert": lax.div(block, dp_axis),
            "dp": lax.rem(block, dp_axis),
            "head": head_index,
        }

    def peer(k):
        other, rest, bit = 0, me, 1
        while bit < blocks:
            digit = lax.rem(rest, 2)
            other = other + bit * (1 - digit if k & bit else digit)
            rest, bit = lax.div(rest, 2), 2 * bit
        return other

    barrier = pltpu.get_barrier_semaphore()
    for k in reversed(range(blocks)):
        if k:
            pl.semaphore_signal(barrier, 1, device_id=device(peer(k), head), device_id_type=MESH)
        pl.semaphore_signal(barrier, 1, device_id=device(peer(k), 1 - head), device_id_type=MESH)

    half_start = pl.multiple_of(head * half_width, half_width)
    loads = [
        pltpu.make_async_copy(src, dst, load_sem.at[i])
        for i, (src, dst) in enumerate(
            (
                (keys, k_v),
                (queries, q_v),
                (lengths, lengths_v),
                (new_key, nk_v),
                (new_value, nv_v),
                (values, v_v),
                (w_out, wo_v),
                (resid, res_v),
                (gain.at[:, pl.ds(half_start, half_width)], gain_v),
                (routes, routes_v),
                (router.at[pl.ds(half_start, half_width), :], rt_v),
                (w_gate, wg_v),
                (w_up, wu_v),
                (w_down, wd_v),
            )
        )
    ]
    for load in loads[:6]:
        load.start()
    (ld_k, ld_q, ld_len, ld_nk, ld_nv, ld_v, ld_wo, ld_res, ld_gain, ld_routes, ld_rt, ld_wg, ld_wu, ld_wd) = loads

    cached = keys.shape[1]
    scale = head_size ** (-0.5)
    column = lax.broadcasted_iota(jnp.int32, (heads_dev, cached), 1)
    head_of = lax.broadcasted_iota(jnp.int32, (heads_dev, cached), 0)
    position = lax.div(column, kv_dev)
    same_kv = lax.rem(column, kv_dev) == lax.div(head_of, group_size)
    kv_of = lax.div(lax.broadcasted_iota(jnp.int32, (heads_dev, head_size), 0), group_size)
    ld_q.wait()
    ld_len.wait()
    ld_nk.wait()
    ld_nv.wait()
    ld_k.wait()
    for load in loads[6:]:
        load.start()
    each = range(rows_dev)
    scores = [
        lax.dot_general(q_v[r], k_v[r], (((1,), (1,)), ((), ())), preferred_element_type=F32)
        for r in each
    ]
    fresh_keys, fresh_values = [], []
    for r in each:
        fresh_key = jnp.zeros((heads_dev, head_size), F32)
        fresh_value = jnp.zeros((heads_dev, head_size), F32)
        for k in range(kv_dev):
            fresh_key = jnp.where(kv_of == k, nk_v[r, k : k + 1, :].astype(F32), fresh_key)
            fresh_value = jnp.where(kv_of == k, nv_v[r, k : k + 1, :].astype(F32), fresh_value)
        fresh_keys.append(fresh_key)
        fresh_values.append(fresh_value)
    score_new = [
        jnp.sum(q_v[r].astype(F32) * fresh_keys[r], axis=-1, keepdims=True) * scale for r in each
    ]
    scores = [
        jnp.where(same_kv & (position < lengths_v[r]), scores[r] * scale, -jnp.inf) for r in each
    ]
    highest = [
        jnp.maximum(jnp.max(scores[r], axis=-1, keepdims=True), score_new[r]) for r in each
    ]
    exp_cache = [jnp.exp(scores[r] - highest[r]) for r in each]
    exp_new = [jnp.exp(score_new[r] - highest[r]) for r in each]
    inverse = [
        1.0 / (jnp.sum(exp_cache[r], axis=-1, keepdims=True) + exp_new[r]) for r in each
    ]
    probs = [(exp_cache[r] * inverse[r]).astype(BF16) for r in each]
    probs_new = [(exp_new[r] * inverse[r]).astype(BF16).astype(F32) for r in each]
    pl.semaphore_wait(barrier, 2 * blocks - 1)

    def exchange(r, k):
        to = peer(k)
        return pltpu.make_async_remote_copy(
            src_ref=attn_all.at[me, pl.ds(r * heads_dev, heads_dev)],
            dst_ref=attn_all.at[me, pl.ds(r * heads_dev, heads_dev)],
            send_sem=attn_ssem.at[r * blocks + to],
            recv_sem=attn_rsem.at[r * blocks + me],
            device_id=device(to, head),
            device_id_type=MESH,
        )

    def arrival(src, dst, ssem, rsem, block):
        return pltpu.make_async_remote_copy(
            src_ref=src,
            dst_ref=dst,
            send_sem=ssem.at[block],
            recv_sem=rsem.at[block],
            device_id=device(lax.rem(block, blocks), head),
            device_id_type=MESH,
        )

    def to_sibling(src, dst, i):
        return pltpu.make_async_remote_copy(
            src_ref=src,
            dst_ref=dst,
            send_sem=pair_ssem.at[i],
            recv_sem=pair_rsem.at[i],
            device_id=device(me, 1 - head),
            device_id_type=MESH,
        )

    ld_v.wait()
    sends = []
    for r in each:
        mixed = jnp.dot(probs[r], v_v[r], preferred_element_type=F32)
        attn = mixed + probs_new[r] * fresh_values[r]
        attn_all[me, r * heads_dev : (r + 1) * heads_dev, :] = attn.astype(BF16)
        row_sends = [exchange(r, k) for k in reversed(range(1, blocks))]
        for copy in row_sends:
            copy.start()
        sends += row_sends
    block_rows = rows_dev * heads_dev

    def widen(block):
        start = pl.multiple_of(block * block_rows, block_rows)
        attn_f32[pl.ds(start, block_rows), :] = attn_all[block].astype(F32)

    widen(me)

    ld_routes.wait()
    expert_ids = lax.broadcasted_iota(jnp.int32, (rows, router.shape[1]), 1)
    row_is_lane = lax.broadcasted_iota(jnp.int32, (rows, rows), 0) == lax.broadcasted_iota(
        jnp.int32, (rows, rows), 1
    )

    def pick(k):
        return jnp.sum(jnp.where(row_is_lane, routes_v[k : k + 1, :], 0), axis=1, keepdims=True)

    own = pick(0)
    picked = expert_ids == own
    for k in range(1, routes.shape[0]):
        chosen = pick(k)
        picked = picked | (expert_ids == chosen)
        own = jnp.minimum(own, chosen)
    is_mine = own == expert

    for k in range(1, blocks):
        block = peer(k)
        for r in each:
            row = attn_all.at[block, pl.ds(r * heads_dev, heads_dev)]
            arrival(row, row, attn_ssem, attn_rsem, r * blocks + block).wait_recv()
        widen(block)
    for h in range(heads_dev):
        attn_mat[:, h * head_size : (h + 1) * head_size] = attn_f32[
            pl.ds(h, rows, stride=heads_dev), :
        ].astype(BF16)

    ld_wo.wait()
    proj_mine[...] = jnp.dot(attn_mat[...], wo_v[...], preferred_element_type=F32)
    proj_copy = to_sibling(proj_mine, proj_other, 0)
    proj_copy.start()
    ld_res.wait()
    ld_gain.wait()
    proj_copy.wait_recv()
    hidden = (res_v[...].astype(F32) + (proj_mine[...] + proj_other[...])).astype(BF16)
    hid_send[...] = hidden
    half_of = lax.div(me, half_blocks)
    slot = lax.rem(me, half_blocks)
    stays = head == half_of
    target_dp = lax.rem(dp + jnp.where(stays, 0, 1), dp_axis)

    def hid_copy(k):
        to = lax.div(peer(k * dp_axis), dp_axis)
        return pltpu.make_async_remote_copy(
            src_ref=hid_send,
            dst_ref=hid_all.at[slot],
            send_sem=hid_ssem.at[k],
            recv_sem=hid_rsem.at[slot],
            device_id={"expert": to, "dp": target_dp, "head": half_of},
            device_id_type=MESH,
        )

    sq_dp = lax.rem(dp + jnp.where(stays, 1, 0), dp_axis)

    def sq_copy(k):
        to = lax.div(peer(k * dp_axis), dp_axis)
        return pltpu.make_async_remote_copy(
            src_ref=sq_mine,
            dst_ref=sq_all.at[slot],
            send_sem=sq_ssem.at[k],
            recv_sem=sq_rsem.at[slot],
            device_id={"expert": to, "dp": sq_dp, "head": 1 - half_of},
            device_id_type=MESH,
        )

    def lane_squares(block, total):
        for start in range(0, cols, total.shape[1]):
            part = block[:, start : start + total.shape[1]]
            total = total + part * part
        return total

    for k in reversed(range(1, experts_axis)):
        hid_copy(k).start()

    @pl.when(jnp.logical_not(stays))
    def _():
        hid_copy(0).start()

    own_squares = lane_squares(hidden.astype(F32), jnp.zeros(sq_mine.shape, F32))
    sq_mine[...] = own_squares
    for k in reversed(range(1, experts_axis)):
        sq_copy(k).start()

    @pl.when(stays)
    def _():
        sq_copy(0).start()
        hid_all[slot] = hidden

    @pl.when(jnp.logical_not(stays))
    def _():
        sq_all[slot] = own_squares

    for copy in sends + [proj_copy]:
        copy.wait_send()

    for i in range(half_blocks):

        @pl.when(jnp.logical_not(stays & (slot == i)))
        def _():
            pltpu.make_async_remote_copy(
                src_ref=hid_send,
                dst_ref=hid_all.at[i],
                send_sem=hid_ssem.at[0],
                recv_sem=hid_rsem.at[i],
                device_id=device(me, 1 - head),
                device_id_type=MESH,
            ).wait_recv()

    squares = jnp.zeros(sq_mine.shape, F32)
    blocks_f32 = [hid_all[i].astype(F32) for i in range(half_blocks)]
    for block in blocks_f32:
        squares = lane_squares(block, squares)
    for i in range(half_blocks):

        @pl.when(stays | (slot != i))
        def _():
            pltpu.make_async_remote_copy(
                src_ref=sq_mine,
                dst_ref=sq_all.at[i],
                send_sem=sq_ssem.at[0],
                recv_sem=sq_rsem.at[i],
                device_id=device(me, 1 - head),
                device_id_type=MESH,
            ).wait_recv()

        squares = squares + sq_all[i]
    row_index = lax.broadcasted_iota(jnp.int32, (rows, 1), 0)
    is_own_row = lax.div(row_index, rows_dev) == me
    kept = [jnp.where(is_own_row, block, 0.0) for block in blocks_f32]
    total = jnp.sum(squares, axis=1, keepdims=True)
    inverse_rms = lax.rsqrt(total / (2 * half_width) + 1e-06)
    normed = jnp.concatenate(
        [
            (block * inverse_rms * gain_v[:, i * cols : (i + 1) * cols]).astype(BF16)
            for i, block in enumerate(blocks_f32)
        ],
        axis=1,
    )

    ld_wg.wait()
    gate_mine[...] = jnp.dot(normed, wg_v[...], preferred_element_type=F32)
    gate_copy = to_sibling(gate_mine, gate_other, 1)
    gate_copy.start()
    ld_rt.wait()
    logit_mine[...] = jnp.dot(normed, rt_v[...], preferred_element_type=F32)
    logit_copy = to_sibling(logit_mine, logit_other, 2)
    logit_copy.start()
    ld_wu.wait()
    up_mine[...] = jnp.dot(normed, wu_v[...], preferred_element_type=F32)
    up_copy = to_sibling(up_mine, up_other, 3)
    up_copy.start()

    for k in range(1, experts_axis):
        hid_copy(k).wait_send()
        sq_copy(k).wait_send()

    @pl.when(stays)
    def _():
        sq_copy(0).wait_send()

    @pl.when(jnp.logical_not(stays))
    def _():
        hid_copy(0).wait_send()

    logit_copy.wait_recv()
    logits = jnp.where(picked, logit_mine[...] + logit_other[...], -jnp.inf)
    weights = jnp.exp(logits - jnp.max(logits, axis=1, keepdims=True))
    share = jnp.sum(jnp.where(expert_ids == own, weights, 0.0), axis=1, keepdims=True) / jnp.sum(
        weights, axis=1, keepdims=True
    )
    row_share = jnp.where(is_mine, share, 0.0)
    gate_copy.wait_recv()
    gate = gate_mine[...] + gate_other[...]
    gate = gate / (1.0 + jnp.exp(-gate))
    ld_wd.wait()
    up_copy.wait_recv()
    activated = (gate * (up_mine[...] + up_other[...])).astype(BF16)
    routed = jnp.dot(activated, wd_v[...], preferred_element_type=F32) * row_share
    routed = routed + jnp.concatenate(kept, axis=1)
    piece = y_mine.shape[2]
    for block in range(blocks):
        for i in range(half_width // piece):
            y_mine[block, i * rows_dev : (i + 1) * rows_dev, :] = routed[
                block * rows_dev : (block + 1) * rows_dev, i * piece : (i + 1) * piece
            ]
        y_send[block] = y_mine[block].astype(BF16)

    y_sends = []
    for k in reversed(range(1, blocks)):
        to = peer(k)
        y_sends.append(
            pltpu.make_async_remote_copy(
                src_ref=y_send.at[to],
                dst_ref=y_recv.at[me],
                send_sem=y_ssem.at[to],
                recv_sem=y_rsem.at[me],
                device_id=device(to, head),
                device_id_type=MESH,
            )
        )
    for copy in y_sends:
        copy.start()
    result = y_mine[me]
    for k in range(1, blocks):
        block = peer(k)
        arrival(y_send.at[block], y_recv.at[block], y_ssem, y_rsem, block).wait_recv()
        result = result + y_recv[block].astype(F32)
    for i in range(half_width // piece):
        out[:, i * piece : (i + 1) * piece] = result[i * rows_dev : (i + 1) * rows_dev, :]
    for copy in [gate_copy, logit_copy, up_copy] + y_sends:
        copy.wait_send()


def body(
    experts_axis,
    dp_axis,
    queries,
    new_key,
    new_value,
    key_cache,
    value_cache,
    lengths,
    w_out,
    resid_cols,
    norm_gain,
    router,
    routes,
    capacity_slot,
    w_gate,
    w_up,
    w_down,
):
    blocks = experts_axis * dp_axis
    rows_dev, heads_dev, head_size = queries.shape
    cache_len, kv_dev = key_cache.shape[1:3]
    rows = rows_dev * blocks
    cols = w_out.shape[1]
    half_width, ff_dev = w_gate.shape[1:]
    names = router.shape[1]
    if cols % 128 or ff_dev % 128 or rows > 64 or rows % 16 or blocks & (blocks - 1) or dp_axis != 2 or rows_dev != 2:
        return plain_body(
            queries,
            new_key,
            new_value,
            key_cache,
            value_cache,
            lengths,
            w_out,
            resid_cols,
            norm_gain,
            router,
            routes,
            capacity_slot,
            w_gate,
            w_up,
            w_down,
        )
    half_blocks = blocks // 2
    tile = 16
    dma = pltpu.SemaphoreType.DMA
    vmem_spec = pl.BlockSpec(memory_space=pltpu.VMEM)
    cached = cache_len * kv_dev
    scratch = [
        pltpu.VMEM((rows_dev, heads_dev, head_size), BF16),
        pltpu.SMEM((rows_dev,), jnp.int32),
        pltpu.VMEM(new_key.shape, BF16),
        pltpu.VMEM(new_value.shape, BF16),
        pltpu.VMEM((rows_dev, cached, head_size), BF16),
        pltpu.VMEM((rows_dev, cached, head_size), BF16),
        pltpu.VMEM(w_out.shape, BF16),
        pltpu.VMEM(resid_cols.shape, BF16),
        pltpu.VMEM((1, half_width), F32),
        pltpu.VMEM((half_width, names), BF16),
        pltpu.VMEM(routes.shape[::-1], jnp.int32),
        pltpu.VMEM((half_width, ff_dev), BF16),
        pltpu.VMEM((half_width, ff_dev), BF16),
        pltpu.VMEM((ff_dev, half_width), BF16),
        pltpu.VMEM((blocks, rows_dev * heads_dev, head_size), BF16),
        pltpu.VMEM((rows * heads_dev, head_size), F32),
        pltpu.VMEM((rows, heads_dev * head_size), BF16),
        pltpu.VMEM((rows, cols), F32),
        pltpu.VMEM((rows, cols), F32),
        pltpu.VMEM((rows, cols), BF16),
        pltpu.VMEM((half_blocks, rows, cols), BF16),
        pltpu.VMEM((rows, 128), F32),
        pltpu.VMEM((half_blocks, rows, 128), F32),
        pltpu.VMEM((rows, ff_dev), F32),
        pltpu.VMEM((rows, ff_dev), F32),
        pltpu.VMEM((rows, ff_dev), F32),
        pltpu.VMEM((rows, ff_dev), F32),
        pltpu.VMEM((rows, names), F32),
        pltpu.VMEM((rows, names), F32),
        pltpu.VMEM((blocks, tile, rows_dev * half_width // tile), F32),
        pltpu.VMEM((blocks, tile, rows_dev * half_width // tile), BF16),
        pltpu.VMEM((blocks, tile, rows_dev * half_width // tile), BF16),
        dma((14,)),
        dma((rows_dev * blocks,)),
        dma((rows_dev * blocks,)),
        dma((experts_axis,)),
        dma((half_blocks,)),
        dma((experts_axis,)),
        dma((half_blocks,)),
        dma((4,)),
        dma((4,)),
        dma((blocks,)),
        dma((blocks,)),
    ]
    out = pl.pallas_call(
        functools.partial(step_kernel, experts_axis, dp_axis),
        out_shape=pltpu.VMEM((rows_dev, half_width), F32),
        in_specs=[pl.BlockSpec(memory_space=pl.ANY)] * 14,
        out_specs=vmem_spec,
        scratch_shapes=scratch,
        compiler_params=pltpu.CompilerParams(
            collective_id=0, has_side_effects=True, vmem_limit_bytes=60 * 1024 * 1024
        ),
    )(
        lengths,
        queries,
        new_key,
        new_value,
        key_cache.reshape(rows_dev, cached, head_size),
        value_cache.reshape(rows_dev, cached, head_size),
        w_out,
        resid_cols,
        norm_gain[None, :],
        router,
        routes.T,
        w_gate[0],
        w_up[0],
        w_down[0],
    )
    return out.astype(BF16)


def solution(mesh):
    in_specs = (
        P(("groups", "expert", "dp"), "head", None),
        P(("groups", "expert", "dp"), "head", None),
        P(("groups", "expert", "dp"), "head", None),
        P(("groups", "expert", "dp"), None, "head", None),
        P(("groups", "expert", "dp"), None, "head", None),
        P(("groups", "expert", "dp")),
        P("head", ("expert", "dp")),
        P("groups", ("expert", "dp")),
        P(),
        P(),
        P("groups", None),
        P("groups"),
        P("expert", "head", "dp"),
        P("expert", "head", "dp"),
        P("expert", "dp", "head"),
    )
    out_specs = P(("groups", "expert", "dp"), "head")
    return jax.shard_map(
        functools.partial(body, mesh.shape["expert"], mesh.shape["dp"]),
        mesh=mesh, in_specs=in_specs, out_specs=out_specs, check_vma=False)
```
